128 devices in a mesh: img: 16 (over z, x_lo, core), txt: 8 (over x_hi, y).
Axes of the slice: x: 4 (x_hi: 2, x_lo: 2; x = x_hi * 2 + x_lo), y: 4, z: 4, core: 2. Of those that a mesh axis runs over, the one named last changes fastest.
Arguments:
- images: bfloat16 [16384, 1152], P(('img', 'txt')), may hold values from -4 to 4
- texts: bfloat16 [16384, 1152], P(('txt', 'img')), may hold values from -4 to 4
- logit_scale: float32 [1], replicated, may hold values from 1.6 to 2.5
- bias: float32 [1], replicated, may hold values from -8 to -3
Outputs:
- loss: float32 [1], replicated
- image_grad: float32 [16384, 1152], P(('img', 'txt'))
- text_grad: float32 [16384, 1152], P(('txt', 'img'))
The draws below stay inside these ranges and needn't reach their ends.
All inputs are finite; a program needn't handle non-finite values.
Results may differ from the reference program's by a relative error of at most 0.0013.
The reference program's roundings to bfloat16 on the way (of `image_unit`, `text_unit` and `coeff`) count: a program that leaves them out, or rounds other values in their place, can miss the bound.
Values may be sent and summed in bfloat16 or wider, within the bound.
No kernel may reach another device: no remote copies, remote signals or barrier semaphores. Data moves between devices by JAX's collectives and lax.ppermute only.
A program may use at most 64 MiB of HBM per device.

```python
import jax
import jax.numpy as jnp
from jax import lax

D = 1152
N = 16384


def shared_base(key):
    base = jax.random.normal(key, (N, D), jnp.float32)
    return base


def scaled_rows(key, base, low, high):
    own = jax.random.normal(key, (N, D), jnp.float32)
    spread = jnp.exp(jax.random.uniform(jax.random.fold_in(key, 3), (N, 1), jnp.float32, jnp.log(low), jnp.log(high)))
    return (base + 0.6 * own) * spread / jnp.sqrt(D * 1.0)


def draw_images(key, part):
    base = shared_base(key)
    low, high = (0.3, 1.0)
    key = jax.random.fold_in(key, 1)
    return jnp.clip(scaled_rows(key, base, low, high), -4.0, 4.0).astype(jnp.bfloat16)


def draw_texts(key, part):
    base = shared_base(key)
    low, high = (0.3, 1.0)
    key = jax.random.fold_in(key, 2)
    return jnp.clip(scaled_rows(key, base, low, high), -4.0, 4.0).astype(jnp.bfloat16)


def setup_inputs(seed: int = 0) -> dict:
    seeds = jax.random.split(jax.random.key(seed), 5)
    return {
        "images": draw_images(jax.random.fold_in(seeds[4], 71), 0),
        "texts": draw_texts(jax.random.fold_in(seeds[4], 71), 0),
        "logit_scale": jnp.clip(jax.random.uniform(seeds[2], (1,), jnp.float32, 1.6, 2.5), 1.6, 2.5),
        "bias": jnp.clip(jax.random.uniform(seeds[3], (1,), jnp.float32, -8.0, -3.0), -8.0, -3.0),
    }


def unit_rows(raw):
    wide = raw.astype(jnp.float32)
    inverse = lax.rsqrt(lax.optimization_barrier(jnp.sum(wide * wide, axis=1, keepdims=True)) + 1e-06)
    return (inverse, wide * inverse)

def back_norm(inverse, unit_wide, grad):
    return inverse * (grad - unit_wide * lax.optimization_barrier(jnp.sum(unit_wide * grad, axis=1, keepdims=True)))

def reference(images, texts, logit_scale, bias):
    temper = jnp.exp(logit_scale[0])
    shift = bias[0]
    image_inv, image_wide = unit_rows(images)
    text_inv, text_wide = unit_rows(texts)
    image_unit = image_wide.astype(jnp.bfloat16).astype(jnp.float32)
    text_unit = text_wide.astype(jnp.bfloat16).astype(jnp.float32)
    block_rows = 512 if N % 512 == 0 else N
    count = N // block_rows
    image_blocks = image_unit.reshape(count, block_rows, D)
    columns = jnp.arange(N, dtype=jnp.int32)[None, :]

    def visit(carry, item):
        loss_sum, text_acc = carry
        block, index = item
        logits = temper * jnp.dot(block, text_unit.T, preferred_element_type=jnp.float32) + shift
        rows = index * block_rows + jnp.arange(block_rows, dtype=jnp.int32)[:, None]
        sign = jnp.where(rows == columns, 1.0, -1.0).astype(jnp.float32)
        loss_sum = loss_sum - jnp.sum(jax.nn.log_sigmoid(sign * logits))
        coeff = (-sign * jax.nn.sigmoid(-sign * logits) * temper).astype(jnp.bfloat16).astype(jnp.float32)
        image_part = jnp.dot(coeff, text_unit, preferred_element_type=jnp.float32)
        text_acc = text_acc + jnp.dot(coeff.T, block, preferred_element_type=jnp.float32)
        return ((loss_sum, text_acc), image_part)
    start = (jnp.zeros((), jnp.float32), jnp.zeros((N, D), jnp.float32))
    indices = jnp.arange(count, dtype=jnp.int32)
    (loss_sum, unit_text_grad), parts = lax.scan(visit, start, (image_blocks, indices))
    unit_image_grad = parts.reshape(N, D)
    image_grad = back_norm(image_inv, image_wide, unit_image_grad)
    text_grad = back_norm(text_inv, text_wide, unit_text_grad)
    loss = (loss_sum / N).reshape(1)
    return (loss, image_grad, text_grad)
```

```python
import functools

import jax
import jax.numpy as jnp
from jax import lax
from jax.experimental import pallas as pl
from jax.experimental.pallas import tpu as pltpu
from jax.sharding import PartitionSpec as P

IMG = (4, 2, 2)
TXT = (2, 4)
PIECE = 128
LOG2E = 1.4426950408889634
LN2 = 0.6931471805599453
NT = (((1,), (1,)), ((), ()))
NN = (((1,), (0,)), ((), ()))
TN = (((0,), (0,)), ((), ()))
HBM = pl.BlockSpec(memory_space=pl.ANY)
SMEM = pl.BlockSpec(memory_space=pltpu.SMEM)
VMEM = pl.BlockSpec(memory_space=pltpu.VMEM)


def index_of(coords, sizes):
    flat = 0
    for coord, size in zip(coords, sizes):
        flat = flat * size + coord % size
    return flat


def from_offset(value, axis, sizes, offset):
    pairs = []
    grid = [()]
    for size in sizes:
        grid = [g + (k,) for g in grid for k in range(size)]
    for coords in grid:
        source = tuple(c + o for c, o in zip(coords, offset))
        pairs.append((index_of(source, sizes), index_of(coords, sizes)))
    return lax.ppermute(value, axis, pairs)


def from_img(value, z=0, x=0, core=0):
    return from_offset(value, "img", IMG, (z, x, core))


def from_txt(value, x=0, y=0):
    return from_offset(value, "txt", TXT, (x, y))


def encode(value):
    square = value * value
    return ((square * value) * (square * square)).astype(jnp.bfloat16)


def decode(code):
    wide = code.astype(jnp.float32)
    size = jnp.abs(wide)
    root = jnp.exp(jnp.log(jnp.maximum(size, 1e-38)) * (1.0 / 7.0))
    return jnp.where(size < 1e-38, 0.0, jnp.where(wide < 0.0, -root, root))


def unit_kernel(images_ref, texts_ref, image_unit_ref, text_unit_ref):
    for raw_ref, unit_ref in ((images_ref, image_unit_ref), (texts_ref, text_unit_ref)):
        wide = raw_ref[...].astype(jnp.float32)
        inverse = lax.rsqrt(jnp.sum(wide * wide, axis=1, keepdims=True) + 1e-06)
        unit_ref[...] = (wide * inverse).astype(jnp.bfloat16)


def unit_rows(images, texts):
    shape = jax.ShapeDtypeStruct(images.shape, jnp.bfloat16)
    return pl.pallas_call(
        unit_kernel,
        out_shape=[shape, shape],
        in_specs=[VMEM, VMEM],
        out_specs=[VMEM, VMEM],
        name="unit_rows",
    )(images, texts)


def pair_kernel(width, chunk, place_ref, scale_ref, bias_ref, *refs):
    image_refs, text_refs, text_rest = refs[:8], refs[8:16], refs[16]
    image_outs, text_own, text_other, loss_ref = refs[17:25], refs[25], refs[26], refs[27]
    image_all, text_all, total, coeff_ref, own_part, other_part, image_code, in_sem, out_sem = refs[28:]
    height = image_all.shape[0]
    half = text_rest.shape[0]
    loads = [
        pltpu.make_async_copy(ref, image_all.at[pl.ds(p * PIECE, PIECE), :], in_sem.at[p])
        for p, ref in enumerate(image_refs)
    ]
    loads += [
        pltpu.make_async_copy(ref, text_all.at[pl.ds(p * PIECE, PIECE), :], in_sem.at[8 + p])
        for p, ref in enumerate(text_refs)
    ]
    loads.append(pltpu.make_async_copy(text_rest, text_all.at[pl.ds(half, half), :], in_sem.at[16]))
    for load in loads:
        load.start()
    for load in loads[:8]:
        load.wait()

    z, x_lo, core, x_hi, y = (place_ref[k] for k in range(5))
    img = (z * 2 + x_lo) * 2 + core
    txt = x_hi * 4 + y
    image_base = [
        (img * 8 + lax.rem(x_hi + p // 4, 2) * 4 + lax.rem(y + p % 4, 4)) * PIECE for p in range(8)
    ]
    text_base = [
        (
            txt * 16
            + lax.rem(z + (p % 8) % 4, 4) * 4
            + lax.rem(x_lo + (p % 8) // 4, 2) * 2
            + lax.rem(core + p // 8, 2)
        )
        * PIECE
        for p in range(16)
    ]
    temper = jnp.exp(jnp.full((1, PIECE), scale_ref[0], jnp.float32))
    slope = temper * LOG2E
    shift = jnp.full((1, PIECE), bias_ref[0] * LOG2E, jnp.float32)
    apart = lax.broadcasted_iota(jnp.int32, (PIECE, PIECE), 0) - lax.broadcasted_iota(
        jnp.int32, (PIECE, PIECE), 1
    )
    quarter = PIECE // 4
    loss_sum = jnp.zeros((8, PIECE), jnp.float32)
    own_sum = jnp.zeros((8, PIECE), jnp.float32)
    stores = []
    for tile in range(2 * half // width):
        first = tile * width // PIECE
        if first < 8:
            for load in loads[8 + first : 8 + first + width // PIECE]:
                load.wait()
        elif first == 8:
            loads[16].wait()
        texts = text_all[tile * width : (tile + 1) * width, :]
        for r in range(height // chunk):
            dots = lax.dot_general(
                image_all[r * chunk : (r + 1) * chunk, :], texts, NT, preferred_element_type=jnp.float32
            )
            for a in range(chunk // PIECE):
                for b in range(width // PIECE):
                    rows = slice(a * PIECE, (a + 1) * PIECE)
                    cols = slice(b * PIECE, (b + 1) * PIECE)
                    power = dots[rows, cols] * slope + shift
                    grown = jnp.exp2(power)
                    pair = apart == text_base[first + b] - image_base[r * (chunk // PIECE) + a]
                    weight = jnp.where(pair, -1.0, grown) * pl.reciprocal(1.0 + grown) * temper
                    coeff_ref[r * chunk + a * PIECE : r * chunk + (a + 1) * PIECE, cols] = weight.astype(
                        jnp.bfloat16
                    )
                    g = [grown[k * quarter : (k + 1) * quarter] for k in range(4)]
                    low = g[0] + g[1] + g[0] * g[1]
                    high = g[2] + g[3] + g[2] * g[3]
                    terms = jnp.log(1.0 + (low + high + low * high))
                    chosen = jnp.where(pair, power, 0.0)
                    for k in range(quarter // 8):
                        loss_sum = loss_sum + terms[k * 8 : (k + 1) * 8]
                    for k in range(PIECE // 8):
                        own_sum = own_sum + chosen[k * 8 : (k + 1) * 8]
        coeff = coeff_ref[...]
        image_part = lax.dot_general(coeff, texts, NN, preferred_element_type=jnp.float32)
        total[...] = image_part if tile == 0 else total[...] + image_part
        text_part = lax.dot_general(coeff, image_all[...], TN, preferred_element_type=jnp.float32)
        if tile * width < half:
            kept = own_part.at[pl.ds(tile * width, width), :]
            out = text_own.at[pl.ds(tile * width, width), :]
            kept[...] = text_part
        else:
            kept = other_part.at[pl.ds(tile * width - half, width), :]
            out = text_other.at[pl.ds(tile * width - half, width), :]
            kept[...] = encode(text_part)
        stores.append(pltpu.make_async_copy(kept, out, out_sem.at[8 + tile]))
        stores[-1].start()
    for p in range(1, 8):
        image_code[(p - 1) * PIECE : p * PIECE, :] = encode(total[p * PIECE : (p + 1) * PIECE, :])
    sources = [total.at[pl.ds(0, PIECE), :]] + [
        image_code.at[pl.ds((p - 1) * PIECE, PIECE), :] for p in range(1, 8)
    ]
    for p in range(8):
        stores.append(pltpu.make_async_copy(sources[p], image_outs[p], out_sem.at[p]))
        stores[-1].start()
    loss_ref[...] = loss_sum - LN2 * own_sum
    for store in stores:
        store.wait()


def pair_terms(place, logit_scale, bias, image_pieces, text_pieces, text_rest):
    depth = text_rest.shape[1]
    height, half = PIECE * 8, text_rest.shape[0]
    width, chunk = 512, 256
    wide = jax.ShapeDtypeStruct((PIECE, depth), jnp.float32)
    code = jax.ShapeDtypeStruct((PIECE, depth), jnp.bfloat16)
    outs = pl.pallas_call(
        functools.partial(pair_kernel, width, chunk),
        out_shape=[wide]
        + [code] * 7
        + [
            jax.ShapeDtypeStruct((half, depth), jnp.float32),
            jax.ShapeDtypeStruct((half, depth), jnp.bfloat16),
            jax.ShapeDtypeStruct((8, PIECE), jnp.float32),
        ],
        in_specs=[SMEM, SMEM, SMEM] + [HBM] * 17,
        out_specs=[HBM] * 10 + [VMEM],
        scratch_shapes=[
            pltpu.VMEM((height, depth), jnp.bfloat16),
            pltpu.VMEM((2 * half, depth), jnp.bfloat16),
            pltpu.VMEM((height, depth), jnp.float32),
            pltpu.VMEM((height, width), jnp.bfloat16),
            pltpu.VMEM((half, depth), jnp.float32),
            pltpu.VMEM((half, depth), jnp.bfloat16),
            pltpu.VMEM((height - PIECE, depth), jnp.bfloat16),
            pltpu.SemaphoreType.DMA((17,)),
            pltpu.SemaphoreType.DMA((8 + 2 * half // width,)),
        ],
        compiler_params=pltpu.CompilerParams(vmem_limit_bytes=48 * 2**20),
        cost_estimate=pl.CostEstimate(
            flops=6 * height * 2 * half * depth, bytes_accessed=20 * 2**20, transcendentals=0
        ),
        name="pair_terms",
    )(place, logit_scale, bias, *image_pieces, *text_pieces, text_rest)
    return outs[:8], outs[8], outs[9], outs[10]


def join_kernel(own_ref, other_ref, *out_refs):
    for p, out_ref in enumerate(out_refs):
        rows = slice(p * PIECE, (p + 1) * PIECE)
        total = own_ref[rows, :] + decode(other_ref[rows, :])
        out_ref[...] = total if out_ref.dtype == jnp.float32 else encode(total)


def join_cores(own, other):
    depth = own.shape[1]
    return pl.pallas_call(
        join_kernel,
        out_shape=[jax.ShapeDtypeStruct((PIECE, depth), jnp.float32)]
        + [jax.ShapeDtypeStruct((PIECE, depth), jnp.bfloat16)] * 7,
        in_specs=[VMEM, VMEM],
        out_specs=[VMEM] * 8,
        compiler_params=pltpu.CompilerParams(vmem_limit_bytes=48 * 2**20),
        name="join_cores",
    )(own, other)


def fold_kernel(a_ref, b_ref, c_ref, d_ref, out_ref):
    out_ref[...] = encode(
        decode(a_ref[...]) + decode(b_ref[...]) + decode(c_ref[...]) + decode(d_ref[...])
    )


def fold(parts):
    return pl.pallas_call(
        fold_kernel,
        out_shape=jax.ShapeDtypeStruct(parts[0].shape, jnp.bfloat16),
        in_specs=[VMEM] * 4,
        out_specs=VMEM,
        name="fold",
    )(*parts)


def finish_kernel(raw_ref, own_ref, a_ref, b_ref, c_ref, d_ref, out_ref):
    grad = own_ref[...] + decode(a_ref[...]) + decode(b_ref[...]) + decode(c_ref[...]) + decode(d_ref[...])
    wide = raw_ref[...].astype(jnp.float32)
    inverse = lax.rsqrt(jnp.sum(wide * wide, axis=1, keepdims=True) + 1e-06)
    unit = wide * inverse
    out_ref[...] = inverse * (grad - unit * jnp.sum(unit * grad, axis=1, keepdims=True))


def finish(raw, own, parts):
    return pl.pallas_call(
        finish_kernel,
        out_shape=jax.ShapeDtypeStruct(raw.shape, jnp.float32),
        in_specs=[VMEM] * 6,
        out_specs=VMEM,
        name="finish",
    )(raw, own, *parts)


def shards(images, texts, logit_scale, bias):
    img, txt = lax.axis_index("img"), lax.axis_index("txt")
    place = jnp.stack([img // 4, img // 2 % 2, img % 2, txt // 4, txt % 4]).astype(jnp.int32)
    image_unit, text_unit = unit_rows(images, texts)

    image_far = from_txt(image_unit, x=1)
    text_far = from_img(text_unit, x=1)
    near_images = [from_txt(image_unit, y=k) for k in (1, 2, 3)]
    near_texts = [from_img(text_unit, z=k) for k in (1, 2, 3)]
    far_images = [from_txt(image_far, y=k) for k in (1, 2, 3)]
    far_texts = [from_img(text_far, z=k) for k in (1, 2, 3)]
    image_pieces = [image_unit] + near_images + [image_far] + far_images
    text_pieces = [text_unit] + near_texts + [text_far] + far_texts
    text_rest = from_img(jnp.concatenate(text_pieces, axis=0), core=1)

    image_parts, text_own, text_other, loss_tile = pair_terms(
        place, logit_scale, bias, image_pieces, text_pieces, text_rest
    )

    image_fold = fold([image_parts[4]] + [from_txt(image_parts[4 + k], y=-k) for k in (1, 2, 3)])
    text_parts = join_cores(text_own, from_img(text_other, core=1))
    text_fold = fold([text_parts[4]] + [from_img(text_parts[4 + k], z=-k) for k in (1, 2, 3)])
    image_rest = [from_txt(image_parts[k], y=-k) for k in (1, 2, 3)] + [from_txt(image_fold, x=1)]
    text_rest = [from_img(text_parts[k], z=-k) for k in (1, 2, 3)] + [from_img(text_fold, x=1)]
    image_grad = finish(images, image_parts[0], image_rest)
    text_grad = finish(texts, text_parts[0], text_rest)

    total = lax.psum(jnp.sum(loss_tile), ("img", "txt"))
    count = images.shape[0] * lax.axis_size("img") * lax.axis_size("txt")
    return (total / count).reshape(1), image_grad, text_grad


def solution(mesh):
    placed = (P(("img", "txt"), None), P(("txt", "img"), None), P(), P())
    return jax.shard_map(
        shards,
        mesh=mesh,
        in_specs=placed,
        out_specs=(P(), P(("img", "txt"), None), P(("txt", "img"), None)),
        check_vma=False,
    )
```

```python
import functools

import jax
import jax.numpy as jnp
from jax import lax
from jax.experimental import pallas as pl
from jax.experimental.pallas import tpu as pltpu
from jax.sharding import PartitionSpec as P

PIECE = 128
LOG2E = 1.4426950408889634
LN2 = 0.6931471805599453
NT = (((1,), (1,)), ((), ()))
NN = (((1,), (0,)), ((), ()))
TN = (((0,), (0,)), ((), ()))
HBM = pl.BlockSpec(memory_space=pl.ANY)
SMEM = pl.BlockSpec(memory_space=pltpu.SMEM)
VMEM = pl.BlockSpec(memory_space=pltpu.VMEM)


def swap(value, axis, partner):
    return lax.ppermute(value, axis, [(partner(k), k) for k in range(lax.axis_size(axis))])


def swap_core(value):
    return swap(value, "img", lambda k: k ^ 1)


class ImageMoves:
    @staticmethod
    def across(value):
        return swap(value, "txt", lambda k: k ^ 4)

    @staticmethod
    def even(value):
        return swap(value, "txt", lambda k: k ^ 1)

    @staticmethod
    def odd(value):
        return swap(value, "txt", lambda k: k ^ 3)


class TextMoves:
    @staticmethod
    def across(value):
        return swap(value, "img", lambda k: k ^ 2)

    @staticmethod
    def even(value):
        return swap(value, "img", lambda k: k ^ 4)

    @staticmethod
    def odd(value):
        return swap(value, "img", lambda k: k ^ 12)


def gather(unit, moves):
    far = moves.across(unit)
    near_one = jnp.concatenate([unit, moves.even(unit)], axis=0)
    far_one = jnp.concatenate([far, moves.odd(far)], axis=0)
    return [near_one, moves.odd(near_one), far_one, moves.even(far_one)]


def encode(value):
    square = value * value
    return ((square * value) * (square * square)).astype(jnp.bfloat16)


def decode(code):
    wide = code.astype(jnp.float32)
    size = jnp.abs(wide)
    root = jnp.exp(jnp.log(jnp.maximum(size, 1e-38)) * (1.0 / 7.0))
    return jnp.where(size < 1e-38, 0.0, jnp.where(wide < 0.0, -root, root))


def unit_kernel(images_ref, texts_ref, image_unit_ref, text_unit_ref):
    for raw_ref, unit_ref in ((images_ref, image_unit_ref), (texts_ref, text_unit_ref)):
        wide = raw_ref[...].astype(jnp.float32)
        inverse = lax.rsqrt(jnp.sum(wide * wide, axis=1, keepdims=True) + 1e-06)
        unit_ref[...] = (wide * inverse).astype(jnp.bfloat16)


def unit_rows(images, texts):
    shape = jax.ShapeDtypeStruct(images.shape, jnp.bfloat16)
    return pl.pallas_call(
        unit_kernel,
        out_shape=[shape, shape],
        in_specs=[VMEM, VMEM],
        out_specs=[VMEM, VMEM],
        name="unit_rows",
    )(images, texts)


RING = (0, 1, 3, 2, 0, 3, 1, 2)


def pair_kernel(first_half, width, chunk, place_ref, scale_ref, bias_ref, *refs):
    image_refs, text_refs = refs[:4], refs[4:8]
    if first_half:
        total_out, text_out, loss_ref = refs[8:11]
        image_all, text_all, total, coeff_ref, text_code, load_sem, store_sem = refs[11:]
    else:
        total_in, text_in, loss_in = refs[8:11]
        image_outs, text_outs, loss_ref = refs[11:15], refs[15:19], refs[19]
        image_all, text_all, total, coeff_ref, text_code, text_add, text_wide, image_code, load_sem, store_sem = (
            refs[20:]
        )
    height, count = image_all.shape[0], text_all.shape[0]
    pair = 2 * PIECE
    image_loads = [
        pltpu.make_async_copy(ref, image_all.at[pl.ds(k * pair, pair), :], load_sem.at[k])
        for k, ref in enumerate(image_refs)
    ]
    text_loads = [
        pltpu.make_async_copy(ref, text_all.at[pl.ds(k * pair, pair), :], load_sem.at[4 + k])
        for k, ref in enumerate(text_refs)
    ]
    for load in text_loads[: width // pair] + image_loads + text_loads[width // pair :]:
        load.start()
    if not first_half:
        total_load = pltpu.make_async_copy(total_in, total, load_sem.at[8])
        total_load.start()
        add_load = pltpu.make_async_copy(text_in, text_add, load_sem.at[9])
        add_load.start()

    z, x_lo, core, x_hi, y = (place_ref[k] for k in range(5))
    text_core = 1 - core if first_half else core
    img = (z * 2 + x_lo) * 2 + core
    txt = x_hi * 4 + y
    image_base = [
        (img * 8 + lax.bitwise_xor(x_hi, p // 4) * 4 + lax.bitwise_xor(y, RING[p])) * PIECE for p in range(8)
    ]
    text_base = [
        (txt * 16 + lax.bitwise_xor(z, RING[p]) * 4 + lax.bitwise_xor(x_lo, p // 4) * 2 + text_core) * PIECE
        for p in range(8)
    ]
    temper = jnp.exp(jnp.full((1, PIECE), scale_ref[0], jnp.float32))
    slope = temper * LOG2E
    shift = jnp.full((1, PIECE), bias_ref[0] * LOG2E, jnp.float32)
    apart = lax.broadcasted_iota(jnp.int32, (PIECE, PIECE), 0) - lax.broadcasted_iota(
        jnp.int32, (PIECE, PIECE), 1
    )
    quarter = PIECE // 4
    loss_sum = jnp.zeros((8, PIECE), jnp.float32)
    own_sum = jnp.zeros((8, PIECE), jnp.float32)
    stores = []

    def store(source, target):
        stores.append(pltpu.make_async_copy(source, target, store_sem.at[len(stores)]))
        stores[-1].start()

    for tile in range(count // width):
        first = tile * width // PIECE
        for load in text_loads[tile * width // pair : (tile + 1) * width // pair]:
            load.wait()
        texts = text_all[tile * width : (tile + 1) * width, :]
        for r in range(height // chunk):
            if tile == 0:
                image_loads[r].wait()
            dots = lax.dot_general(
                image_all[r * chunk : (r + 1) * chunk, :], texts, NT, preferred_element_type=jnp.float32
            )
            for a in range(chunk // PIECE):
                for b in range(width // PIECE):
                    rows = slice(a * PIECE, (a + 1) * PIECE)
                    cols = slice(b * PIECE, (b + 1) * PIECE)
                    power = dots[rows, cols] * slope + shift
                    grown = jnp.exp2(power)
                    match = apart == text_base[first + b] - image_base[r * (chunk // PIECE) + a]
                    weight = jnp.where(match, -1.0, grown) * pl.reciprocal(1.0 + grown) * temper
                    coeff_ref[r * chunk + a * PIECE : r * chunk + (a + 1) * PIECE, cols] = weight.astype(
                        jnp.bfloat16
                    )
                    g = [grown[k * quarter : (k + 1) * quarter] for k in range(4)]
                    low = g[0] + g[1] + g[0] * g[1]
                    high = g[2] + g[3] + g[2] * g[3]
                    terms = jnp.log(1.0 + (low + high + low * high))
                    chosen = jnp.where(match, power, 0.0)
                    for k in range(quarter // 8):
                        loss_sum = loss_sum + terms[k * 8 : (k + 1) * 8]
                    for k in range(PIECE // 8):
                        own_sum = own_sum + chosen[k * 8 : (k + 1) * 8]
        coeff = coeff_ref[...]
        text_part = lax.dot_general(coeff, image_all[...], TN, preferred_element_type=jnp.float32)
        rows = slice(tile * width, (tile + 1) * width)
        if first_half:
            text_code[rows, :] = encode(text_part)
            store(text_code.at[pl.ds(tile * width, width), :], text_out.at[pl.ds(tile * width, width), :])
        else:
            if tile == 0:
                add_load.wait()
            text_part = text_part + decode(text_add[rows, :])
            kept = slice(tile * pair, (tile + 1) * pair)
            text_wide[kept, :] = text_part[:pair]
            store(text_wide.at[pl.ds(tile * pair, pair), :], text_outs[2 * tile])
            text_code[kept, :] = encode(text_part[pair:])
            store(text_code.at[pl.ds(tile * pair, pair), :], text_outs[2 * tile + 1])
        image_part = lax.dot_general(coeff, texts, NN, preferred_element_type=jnp.float32)
        if tile == 0 and first_half:
            total[...] = image_part
        else:
            if tile == 0:
                total_load.wait()
            total[...] = total[...] + image_part
    loss = loss_sum - LN2 * own_sum
    if first_half:
        store(total, total_out)
        loss_ref[...] = loss
    else:
        for k in range(2):
            code = slice(k * pair, (k + 1) * pair)
            image_code[code, :] = encode(total[(2 * k + 1) * pair : (2 * k + 2) * pair, :])
            store(image_code.at[pl.ds(k * pair, pair), :], image_outs[2 * k + 1])
            store(total.at[pl.ds(2 * k * pair, pair), :], image_outs[2 * k])
        loss_ref[...] = jnp.broadcast_to(jnp.sum(loss + loss_in[...], keepdims=True), loss_ref.shape)
    for copy in stores:
        copy.wait()


def pair_terms(place, logit_scale, bias, images, texts, first=None):
    pair, depth = images[0].shape
    height = count = 4 * pair
    width, chunk = 2 * pair, pair
    tiles = count // width
    wide = jax.ShapeDtypeStruct((pair, depth), jnp.float32)
    code = jax.ShapeDtypeStruct((pair, depth), jnp.bfloat16)
    loss = jax.ShapeDtypeStruct((8, PIECE), jnp.float32)
    scratch = [
        pltpu.VMEM((height, depth), jnp.bfloat16),
        pltpu.VMEM((count, depth), jnp.bfloat16),
        pltpu.VMEM((height, depth), jnp.float32),
        pltpu.VMEM((height, width), jnp.bfloat16),
    ]
    loads, stores = 8, tiles + 1
    if first is None:
        out_shape = [
            jax.ShapeDtypeStruct((height, depth), jnp.float32),
            jax.ShapeDtypeStruct((count, depth), jnp.bfloat16),
            loss,
        ]
        scratch += [pltpu.VMEM((count, depth), jnp.bfloat16)]
        more, more_specs = (), []
    else:
        out_shape = [wide, code] * 4 + [loss]
        scratch += [
            pltpu.VMEM((count // 2, depth), jnp.bfloat16),
            pltpu.VMEM((count, depth), jnp.bfloat16),
            pltpu.VMEM((count // 2, depth), jnp.float32),
            pltpu.VMEM((height // 2, depth), jnp.bfloat16),
        ]
        more, more_specs = first, [HBM, HBM, VMEM]
        loads, stores = 10, 2 * tiles + 4
    return pl.pallas_call(
        functools.partial(pair_kernel, first is None, width, chunk),
        out_shape=out_shape,
        in_specs=[SMEM, SMEM, SMEM] + [HBM] * 8 + more_specs,
        out_specs=[HBM] * (len(out_shape) - 1) + [VMEM],
        scratch_shapes=scratch
        + [pltpu.SemaphoreType.DMA((loads,)), pltpu.SemaphoreType.DMA((stores,))],
        compiler_params=pltpu.CompilerParams(vmem_limit_bytes=40 * 2**20),
        cost_estimate=pl.CostEstimate(
            flops=6 * height * count * depth, bytes_accessed=20 * 2**20, transcendentals=0
        ),
        name="other_texts" if first is None else "own_texts",
    )(place, logit_scale, bias, *images, *texts, *more)


def fold_kernel(near_ref, near_in, far_ref, far_in, near_kept, near_sent, far_kept, far_sent):
    for own, came, kept, sent in (
        (near_ref, near_in, near_kept, near_sent),
        (far_ref, far_in, far_kept, far_sent),
    ):
        sent[...] = encode(own[PIECE:, :] + decode(came[PIECE:, :]))
        kept[...] = own[:PIECE, :] + decode(came[:PIECE, :])


def fold(near, near_in, far, far_in):
    depth = near.shape[1]
    wide = jax.ShapeDtypeStruct((PIECE, depth), jnp.float32)
    code = jax.ShapeDtypeStruct((PIECE, depth), jnp.bfloat16)
    return pl.pallas_call(
        fold_kernel,
        out_shape=[wide, code, wide, code],
        in_specs=[VMEM] * 4,
        out_specs=[VMEM] * 4,
        name="fold",
    )(near, near_in, far, far_in)


def add_kernel(own_ref, came_ref, out_ref):
    out_ref[...] = encode(own_ref[...] + decode(came_ref[...]))


def add_codes(own, came):
    return pl.pallas_call(
        add_kernel,
        out_shape=jax.ShapeDtypeStruct(own.shape, jnp.bfloat16),
        in_specs=[VMEM] * 2,
        out_specs=VMEM,
        name="add_codes",
    )(own, came)


def finish_kernel(raw_ref, own_ref, ring_ref, far_ref, out_ref):
    grad = own_ref[...] + decode(ring_ref[...]) + decode(far_ref[...])
    wide = raw_ref[...].astype(jnp.float32)
    inverse = lax.rsqrt(jnp.sum(wide * wide, axis=1, keepdims=True) + 1e-06)
    unit = wide * inverse
    out_ref[...] = inverse * (grad - unit * jnp.sum(unit * grad, axis=1, keepdims=True))


def finish(raw, own, ring, far):
    return pl.pallas_call(
        finish_kernel,
        out_shape=jax.ShapeDtypeStruct(raw.shape, jnp.float32),
        in_specs=[VMEM] * 4,
        out_specs=VMEM,
        name="finish",
    )(raw, own, ring, far)


def scatter(raw, parts, moves):
    near, near_code, far, far_code = parts
    near_kept, near_sent, far_kept, far_sent = fold(near, moves.odd(near_code), far, moves.even(far_code))
    far_sum = add_codes(far_kept, moves.odd(far_sent))
    return finish(raw, near_kept, moves.even(near_sent), moves.across(far_sum))


def shards(images, texts, logit_scale, bias):
    img, txt = lax.axis_index("img"), lax.axis_index("txt")
    place = jnp.stack([img // 4, img // 2 % 2, img % 2, txt // 4, txt % 4]).astype(jnp.int32)
    image_unit, text_unit = unit_rows(images, texts)
    image_all = gather(image_unit, ImageMoves)
    text_all = gather(text_unit, TextMoves)
    other_all = [swap_core(part) for part in text_all]

    image_total, text_code, loss = pair_terms(place, logit_scale, bias, image_all, other_all)
    parts = pair_terms(
        place, logit_scale, bias, image_all, text_all, (image_total, swap_core(text_code), loss)
    )
    image_grad = scatter(images, parts[:4], ImageMoves)
    text_grad = scatter(texts, parts[4:8], TextMoves)

    total = parts[8]
    for moves in (ImageMoves, TextMoves):
        for move in (moves.even, moves.odd, moves.across):
            total = total + move(total)
    total = total + swap_core(total)
    count = images.shape[0] * lax.axis_size("img") * lax.axis_size("txt")
    return (total[0, :1] / count), image_grad, text_grad


def solution(mesh):
    placed = (P(("img", "txt"), None), P(("txt", "img"), None), P(), P())
    return jax.shard_map(
        shards,
        mesh=mesh,
        in_specs=placed,
        out_specs=(P(), P(("img", "txt"), None), P(("txt", "img"), None)),
        check_vma=False,
    )
```

```python
import functools

import jax
import jax.numpy as jnp
from jax import lax
from jax.experimental import pallas as pl
from jax.experimental.pallas import tpu as pltpu
from jax.sharding import PartitionSpec as P

IMAGE_PAIRS = {"x": 2 << 3, "y": 1, "z": 4 << 3}
TEXT_PAIRS = {"x": (2 << 3) + 4, "y": 3, "z": 12 << 3}
CORE = 1 << 3
PIECE = 128
ROWS = ("", "y", "x", "xz", "z", "yz", "xy", "xyz")
PAIR_VMEM = 28 * 2**20
SMALL_VMEM = 16 * 2**20
LOG2E = 1.4426950408889634
LN2 = 0.6931471805599453
NT = (((1,), (1,)), ((), ()))
NN = (((1,), (0,)), ((), ()))
TN = (((0,), (0,)), ((), ()))
HBM = pl.BlockSpec(memory_space=pl.ANY)
SMEM = pl.BlockSpec(memory_space=pltpu.SMEM)
VMEM = pl.BlockSpec(memory_space=pltpu.VMEM)


def shape_of(rows, depth, dtype):
    return jax.ShapeDtypeStruct((rows, depth), dtype)


def swap(value, mask):
    axes = ("img", "txt")
    return lax.ppermute(value, axes, [(k ^ mask, k) for k in range(lax.axis_size(axes))])


def encode(value):
    square = value * value
    return ((square * value) * (square * square)).astype(jnp.bfloat16)


def decode(code):
    wide = code.astype(jnp.float32)
    root = jnp.exp2(jnp.log2(jnp.abs(wide)) * (1.0 / 7.0))
    return jnp.where(wide < 0.0, -root, root)


def unit_kernel(images_ref, texts_ref, image_out, text_out, raw, sems):
    loads = [pltpu.make_async_copy(ref, raw.at[k], sems.at[k]) for k, ref in enumerate((images_ref, texts_ref))]
    for load in loads:
        load.start()
    for k, out in enumerate((image_out, text_out)):
        loads[k].wait()
        wide = raw[k].astype(jnp.float32)
        inverse = lax.rsqrt(jnp.sum(wide * wide, axis=1, keepdims=True) + 1e-06)
        out[...] = (wide * inverse).astype(jnp.bfloat16)


def unit_rows(images, texts):
    out = shape_of(*images.shape, jnp.bfloat16)
    return pl.pallas_call(
        unit_kernel,
        out_shape=[out, out],
        in_specs=[HBM, HBM],
        out_specs=[VMEM, VMEM],
        scratch_shapes=[pltpu.VMEM((2, *images.shape), jnp.bfloat16), pltpu.SemaphoreType.DMA((2,))],
        compiler_params=pltpu.CompilerParams(vmem_limit_bytes=60 * 2**20),
        name="unit_rows",
    )(images, texts)


def row_masks(pairs):
    return [sum(pairs[axis] for axis in axes) for axes in ROWS]


def logit_kernel(place_ref, scale_ref, bias_ref, *refs):
    image_refs, text_refs = refs[:4], refs[4:12]
    coeff_refs, other_refs, loss_ref = refs[12:14], refs[14:16], refs[16]
    rows = image_refs[0].shape[0]
    pieces = rows // PIECE

    place = place_ref[0]
    image_base = [lax.bitwise_xor(place, mask) * PIECE for mask in row_masks(IMAGE_PAIRS)]
    text_base = []
    for core in (0, CORE):
        for mask in row_masks(TEXT_PAIRS):
            flat = lax.bitwise_xor(place, mask ^ core)
            text_base.append((lax.rem(flat, 8) * 16 + lax.div(flat, 8)) * PIECE)

    temper = jnp.exp(jnp.full((1, PIECE), scale_ref[0], jnp.float32))
    slope = temper * LOG2E
    shift = jnp.full((1, PIECE), bias_ref[0] * LOG2E, jnp.float32)
    apart = lax.broadcasted_iota(jnp.int32, (PIECE, PIECE), 0) - lax.broadcasted_iota(
        jnp.int32, (PIECE, PIECE), 1
    )
    quarter = PIECE // 4
    loss_sum = jnp.zeros((8, PIECE), jnp.float32)
    own_sum = jnp.zeros((8, PIECE), jnp.float32)
    for t in (4, 5, 6, 7, 0, 1, 2, 3):
        coeff_ref, left = coeff_refs[t // 4], t % 4 * rows
        for r, image_ref in enumerate(image_refs):
            dots = lax.dot_general(image_ref[...], text_refs[t][...], NT, preferred_element_type=jnp.float32)
            for a in range(pieces):
                top = r * rows + a * PIECE
                for b in range(pieces):
                    power = dots[a * PIECE : (a + 1) * PIECE, b * PIECE : (b + 1) * PIECE] * slope + shift
                    grown = jnp.exp2(power)
                    match = apart == text_base[t * pieces + b] - image_base[r * pieces + a]
                    weight = jnp.where(match, -1.0, grown) * pl.reciprocal(1.0 + grown) * temper
                    column = left + b * PIECE
                    coeff_ref[top : top + PIECE, column : column + PIECE] = weight.astype(jnp.bfloat16)
                    g = [grown[k * quarter : (k + 1) * quarter] for k in range(4)]
                    low = g[0] + g[1] + g[0] * g[1]
                    high = g[2] + g[3] + g[2] * g[3]
                    terms = jnp.log(1.0 + (low + high + low * high))
                    chosen = jnp.where(match, power, 0.0)
                    for k in range(quarter // 8):
                        loss_sum = loss_sum + terms[k * 8 : (k + 1) * 8]
                    for k in range(PIECE // 8):
                        own_sum = own_sum + chosen[k * 8 : (k + 1) * 8]
        if t >= 4:
            part = text_shares(coeff_ref, left, image_refs)
            other_refs[t % 4 // 2][t % 2 * rows : (t % 2 + 1) * rows, :] = encode(part)
    loss = loss_sum - LN2 * own_sum
    loss_ref[...] = jnp.broadcast_to(jnp.sum(loss, keepdims=True), loss_ref.shape)


def text_shares(coeff_ref, left, image_refs):
    rows = image_refs[0].shape[0]
    part = None
    for r, image_ref in enumerate(image_refs):
        more = lax.dot_general(
            coeff_ref[r * rows : (r + 1) * rows, left : left + rows],
            image_ref[...],
            TN,
            preferred_element_type=jnp.float32,
        )
        part = more if part is None else part + more
    return part


def logit_terms(place, logit_scale, bias, images, texts):
    rows, depth = images[0].shape
    height, count = len(images) * rows, len(texts) * rows
    coeff = shape_of(height, count // 2, jnp.bfloat16)
    outs = pl.pallas_call(
        logit_kernel,
        out_shape=[coeff, coeff]
        + [shape_of(2 * rows, depth, jnp.bfloat16)] * 2
        + [shape_of(8, PIECE, jnp.float32)],
        in_specs=[SMEM, SMEM, SMEM] + [VMEM] * 12,
        out_specs=[VMEM] * 5,
        compiler_params=pltpu.CompilerParams(vmem_limit_bytes=PAIR_VMEM),
        cost_estimate=cost(3 * height * count * depth // 2),
        name="logit_terms",
    )(place, logit_scale, bias, *images, *texts)
    return outs[:2], outs[2:4], outs[4]


def cost(multiplies):
    return pl.CostEstimate(flops=2 * multiplies, bytes_accessed=8 * 2**20, transcendentals=0)


def text_kernel(coeff_ref, *refs):
    image_refs, outs = refs[:4], refs[4:8]
    for t in (2, 3, 0, 1):
        outs[t][...] = text_shares(coeff_ref, t * outs[t].shape[0], image_refs)


def text_terms(coeff, images):
    rows, depth = images[0].shape
    height, count = coeff.shape
    return pl.pallas_call(
        text_kernel,
        out_shape=[shape_of(rows, depth, jnp.float32)] * 4,
        in_specs=[VMEM] * 5,
        out_specs=[VMEM] * 4,
        compiler_params=pltpu.CompilerParams(vmem_limit_bytes=PAIR_VMEM),
        cost_estimate=cost(height * count * depth),
        name="text_terms",
    )(coeff, *images)


def image_kernel(first, own_ref, other_ref, *refs):
    text_refs, outs = refs[:8], refs[8:10]
    rows = outs[0].shape[0]
    for k, out in enumerate(outs):
        top = first + k * rows
        total = None
        for t, text_ref in enumerate(text_refs):
            coeff_ref, left = (own_ref, other_ref)[t // 4], t % 4 * rows
            more = jnp.dot(
                coeff_ref[top : top + rows, left : left + rows], text_ref[...], preferred_element_type=jnp.float32
            )
            total = more if total is None else total + more
        out[...] = total if out.dtype == jnp.float32 else encode(total)


def image_terms(first, dtype, coeffs, texts):
    rows, depth = texts[0].shape
    return pl.pallas_call(
        functools.partial(image_kernel, first),
        out_shape=[shape_of(rows, depth, dtype)] * 2,
        in_specs=[VMEM] * 10,
        out_specs=[VMEM] * 2,
        compiler_params=pltpu.CompilerParams(vmem_limit_bytes=PAIR_VMEM),
        cost_estimate=cost(4 * rows * coeffs[0].shape[1] * depth),
        name="image_terms",
    )(*coeffs, *texts)


def small_call(kernel, name, out_shape, operands):
    return pl.pallas_call(
        kernel,
        out_shape=out_shape,
        in_specs=[VMEM] * len(operands),
        out_specs=[VMEM] * len(out_shape),
        compiler_params=pltpu.CompilerParams(vmem_limit_bytes=SMALL_VMEM),
        name=name,
    )(*operands)


def join_kernel(near_ref, far_ref, came_ref, near_out, far_out, own, came, code, load_sem, store_sem):
    rows = near_ref.shape[0]
    parts = ((1, far_ref, far_out), (0, near_ref, near_out))
    loads, stores = [], []
    for k, own_ref, out in parts:
        place = pl.ds(k * rows, rows)
        loads.append(pltpu.make_async_copy(came_ref.at[place, :], came.at[place, :], load_sem.at[2 * k]))
        loads.append(pltpu.make_async_copy(own_ref, own.at[place, :], load_sem.at[2 * k + 1]))
        stores.append(pltpu.make_async_copy(code.at[place, :], out, store_sem.at[k]))
    for load in loads:
        load.start()
    for n, (k, _, _) in enumerate(parts):
        loads[2 * n].wait()
        loads[2 * n + 1].wait()
        place = pl.ds(k * rows, rows)
        code[place, :] = encode(own[place, :] + decode(came[place, :]))
        stores[n].start()
    for store in stores:
        store.wait()


def join_cores(near, far, came):
    code = shape_of(*near.shape, jnp.bfloat16)
    return pl.pallas_call(
        join_kernel,
        out_shape=[code, code],
        in_specs=[HBM] * 3,
        out_specs=[HBM] * 2,
        scratch_shapes=[
            pltpu.VMEM(came.shape, jnp.float32),
            pltpu.VMEM(came.shape, jnp.bfloat16),
            pltpu.VMEM(came.shape, jnp.bfloat16),
            pltpu.SemaphoreType.DMA((4,)),
            pltpu.SemaphoreType.DMA((2,)),
        ],
        compiler_params=pltpu.CompilerParams(vmem_limit_bytes=PAIR_VMEM),
        name="join_cores",
    )(near, far, came)


def fold_kernel(rows, own_ref, came_ref, *refs):
    core_ref, (kept, sent) = refs[0] if len(refs) == 3 else None, refs[-2:]
    for first, out in ((PIECE, sent), (0, kept)):
        value = own_ref[first : first + PIECE, :] + decode(came_ref[first : first + PIECE, :])
        if core_ref is not None:
            value = value + decode(core_ref[rows + first : rows + first + PIECE, :])
        out[...] = value if out.dtype == jnp.float32 else encode(value)


def fold(own, came, core=None, core_rows=0):
    depth = own.shape[1]
    return small_call(
        functools.partial(fold_kernel, core_rows),
        "fold",
        [shape_of(PIECE, depth, jnp.float32), shape_of(PIECE, depth, jnp.bfloat16)],
        (own, came) if core is None else (own, came, core),
    )


def add_kernel(own_ref, came_ref, out_ref):
    out_ref[...] = encode(own_ref[...] + decode(came_ref[...]))


def add_codes(own, came):
    return small_call(add_kernel, "add_codes", [shape_of(*own.shape, jnp.bfloat16)], (own, came))[0]


def finish_kernel(raw_ref, own_ref, ring_ref, far_ref, out_ref):
    grad = own_ref[...] + decode(ring_ref[...]) + decode(far_ref[...])
    wide = raw_ref[...].astype(jnp.float32)
    inverse = lax.rsqrt(jnp.sum(wide * wide, axis=1, keepdims=True) + 1e-06)
    unit = wide * inverse
    out_ref[...] = inverse * (grad - unit * jnp.sum(unit * grad, axis=1, keepdims=True))


def finish(raw, own, ring, far):
    return small_call(finish_kernel, "finish", [shape_of(*raw.shape, jnp.float32)], (raw, own, ring, far))[0]


def gather(image, text):
    groups = ((image, IMAGE_PAIRS), (text, TEXT_PAIRS))
    far = [swap(unit, pairs["x"]) for unit, pairs in groups]
    *far, image, text = lax.optimization_barrier((*far, image, text))
    groups = ((image, IMAGE_PAIRS), (text, TEXT_PAIRS))
    far = [jnp.concatenate([part, swap(part, pairs["z"])], axis=0) for part, (_, pairs) in zip(far, groups)]
    near = [jnp.concatenate([unit, swap(unit, pairs["y"])], axis=0) for unit, pairs in groups]
    *far, near[0], near[1] = lax.optimization_barrier((*far, *near))
    far_late = [swap(part, pairs["y"]) for part, (_, pairs) in zip(far, groups)]
    near_late = [swap(part, pairs["z"]) for part, (_, pairs) in zip(near, groups)]
    images, texts = ([near[k], far[k], near_late[k], far_late[k]] for k in range(2))
    late_core = [after(far[1], *near_late, *far_late), *texts[2:]]
    return images, texts + [swap(part, CORE) for part in (near[1], *late_core)]


def after(value, *others):
    return lax.optimization_barrier((value, *others))[0]


def shards(images, texts, logit_scale, bias):
    place = (lax.axis_index("img") * lax.axis_size("txt") + lax.axis_index("txt")).astype(jnp.int32)
    image_all, text_all = gather(*unit_rows(images, texts))
    coeffs, other, loss = logit_terms(place.reshape(1), logit_scale, bias, image_all, text_all)

    other_late = swap(other[1], CORE)
    loss = loss + swap(loss, CORE)
    near_late, far_late = image_terms(4 * PIECE, jnp.bfloat16, coeffs, text_all)
    image_far = swap(far_late, IMAGE_PAIRS["y"])
    image_near = swap(near_late, IMAGE_PAIRS["z"])
    own = text_terms(after(coeffs[0], loss, near_late), image_all)
    loss = loss + swap(loss, IMAGE_PAIRS["x"])
    text_near, text_far = join_cores(own[2], own[3], other_late)
    text_far = swap(text_far, TEXT_PAIRS["y"])
    text_near = swap(text_near, TEXT_PAIRS["z"])
    near_early, far_early = image_terms(0, jnp.float32, (after(coeffs[0], loss), coeffs[1]), text_all)
    loss = loss + swap(loss, TEXT_PAIRS["x"])
    other_early = swap(other[0], CORE)

    image_kept, image_sent = fold(far_early, after(image_far, loss))
    image_far = swap(image_sent, IMAGE_PAIRS["z"])
    text_kept, text_sent = fold(own[1], text_far, other_early, 2 * PIECE)
    text_far = swap(text_sent, TEXT_PAIRS["z"])
    loss = loss + swap(loss, IMAGE_PAIRS["y"])
    image_own, image_sent = fold(near_early, image_near)
    image_near = swap(image_sent, IMAGE_PAIRS["y"])
    text_own, text_sent = fold(own[0], text_near, other_early, 0)
    text_near = swap(text_sent, TEXT_PAIRS["y"])

    loss = loss + swap(loss, TEXT_PAIRS["y"])
    image_sent = add_codes(image_kept, after(image_far, loss))
    text_sent = add_codes(text_kept, text_far)
    loss = loss + swap(loss, IMAGE_PAIRS["z"])
    loss = loss + swap(loss, TEXT_PAIRS["z"])
    count = images.shape[0] * lax.axis_size("img") * lax.axis_size("txt")
    loss = loss[0, :1] / count
    image_grad = finish(images, image_own, after(image_near, loss), swap(image_sent, IMAGE_PAIRS["x"]))
    text_grad = finish(texts, text_own, text_near, swap(text_sent, TEXT_PAIRS["x"]))
    return loss, image_grad, text_grad


def solution(mesh):
    placed = (P(("img", "txt"), None), P(("txt", "img"), None), P(), P())
    return jax.shard_map(
        shards,
        mesh=mesh,
        in_specs=placed,
        out_specs=(P(), P(("img", "txt"), None), P(("txt", "img"), None)),
        check_vma=False,
    )
```

```python
import functools

import jax
import jax.numpy as jnp
from jax import lax
from jax.experimental import pallas as pl
from jax.experimental.pallas import tpu as pltpu
from jax.sharding import PartitionSpec as P

IMAGE_PAIRS = {"x": 2 << 3, "y": 1, "z": 4 << 3}
TEXT_PAIRS = {"x": (2 << 3) + 4, "y": 3, "z": 12 << 3}
CORE = 1 << 3
PIECE = 128
ROWS = ("", "y", "x", "xz", "z", "yz", "xy", "xyz")
PAIR_VMEM = 12 * 2**20
SMALL_VMEM = 8 * 2**20
LOG2E = 1.4426950408889634
LN2 = 0.6931471805599453
NT = (((1,), (1,)), ((), ()))
NN = (((1,), (0,)), ((), ()))
TN = (((0,), (0,)), ((), ()))
HBM = pl.BlockSpec(memory_space=pl.ANY)
SMEM = pl.BlockSpec(memory_space=pltpu.SMEM)
VMEM = pl.BlockSpec(memory_space=pltpu.VMEM)


def shape_of(rows, depth, dtype):
    return jax.ShapeDtypeStruct((rows, depth), dtype)


def swap(value, mask):
    axes = ("img", "txt")
    return lax.ppermute(value, axes, [(k ^ mask, k) for k in range(lax.axis_size(axes))])


def encode(value):
    square = value * value
    return ((square * value) * (square * square)).astype(jnp.bfloat16)


def decode(code):
    wide = code.astype(jnp.float32)
    root = jnp.exp2(jnp.log2(jnp.abs(wide)) * (1.0 / 7.0))
    return jnp.where(wide < 0.0, -root, root)


def unit_kernel(images_ref, texts_ref, image_out, text_out, raw, sems):
    loads = [pltpu.make_async_copy(ref, raw.at[k], sems.at[k]) for k, ref in enumerate((images_ref, texts_ref))]
    for load in loads:
        load.start()
    for k, out in enumerate((image_out, text_out)):
        loads[k].wait()
        wide = raw[k].astype(jnp.float32)
        inverse = lax.rsqrt(jnp.sum(wide * wide, axis=1, keepdims=True) + 1e-06)
        out[...] = (wide * inverse).astype(jnp.bfloat16)


def unit_rows(images, texts):
    out = shape_of(*images.shape, jnp.bfloat16)
    return pl.pallas_call(
        unit_kernel,
        out_shape=[out, out],
        in_specs=[HBM, HBM],
        out_specs=[VMEM, VMEM],
        scratch_shapes=[pltpu.VMEM((2, *images.shape), jnp.bfloat16), pltpu.SemaphoreType.DMA((2,))],
        compiler_params=pltpu.CompilerParams(vmem_limit_bytes=60 * 2**20),
        name="unit_rows",
    )(images, texts)


def row_masks(pairs):
    return [sum(pairs[axis] for axis in axes) for axes in ROWS]


def logit_kernel(core, loss_scale, place_ref, scale_ref, bias_ref, *refs):
    image_refs, text_refs = refs[:4], refs[4:8]
    if core:
        loss_in, coeff_ref, other_refs, loss_ref = refs[8], refs[9], refs[10:12], refs[12]
    else:
        coeff_ref, loss_ref = refs[8:]
    rows = image_refs[0].shape[0]
    pieces = rows // PIECE

    place = place_ref[0]
    image_base = [lax.bitwise_xor(place, mask) * PIECE for mask in row_masks(IMAGE_PAIRS)]
    text_base = []
    for mask in row_masks(TEXT_PAIRS):
        flat = lax.bitwise_xor(place, mask ^ core)
        text_base.append((lax.rem(flat, 8) * 16 + lax.div(flat, 8)) * PIECE)

    temper = jnp.exp(jnp.full((1, PIECE), scale_ref[0], jnp.float32))
    slope = temper * LOG2E
    shift = jnp.full((1, PIECE), bias_ref[0] * LOG2E, jnp.float32)
    apart = lax.broadcasted_iota(jnp.int32, (PIECE, PIECE), 0) - lax.broadcasted_iota(
        jnp.int32, (PIECE, PIECE), 1
    )
    quarter = PIECE // 4
    loss_sum = jnp.zeros((8, PIECE), jnp.float32)
    own_sum = jnp.zeros((8, PIECE), jnp.float32)
    for t in (2, 3, 0, 1):
        left = t * rows
        for r, image_ref in enumerate(image_refs):
            dots = lax.dot_general(image_ref[...], text_refs[t][...], NT, preferred_element_type=jnp.float32)
            for a in range(pieces):
                top = r * rows + a * PIECE
                for b in range(pieces):
                    power = dots[a * PIECE : (a + 1) * PIECE, b * PIECE : (b + 1) * PIECE] * slope + shift
                    grown = jnp.exp2(power)
                    match = apart == text_base[t * pieces + b] - image_base[r * pieces + a]
                    weight = jnp.where(match, -1.0, grown) * pl.reciprocal(1.0 + grown) * temper
                    column = left + b * PIECE
                    coeff_ref[top : top + PIECE, column : column + PIECE] = weight.astype(jnp.bfloat16)
                    g = [grown[k * quarter : (k + 1) * quarter] for k in range(4)]
                    low = g[0] + g[1] + g[0] * g[1]
                    high = g[2] + g[3] + g[2] * g[3]
                    terms = jnp.log(1.0 + (low + high + low * high))
                    chosen = jnp.where(match, power, 0.0)
                    for k in range(quarter // 8):
                        loss_sum = loss_sum + terms[k * 8 : (k + 1) * 8]
                    for k in range(PIECE // 8):
                        own_sum = own_sum + chosen[k * 8 : (k + 1) * 8]
        if core:
            other_refs[t // 2][t % 2 * rows : (t % 2 + 1) * rows, :] = encode(
                text_shares(coeff_ref, left, image_refs)
            )
    loss = loss_sum - LN2 * own_sum
    if core:
        total = jnp.sum(loss + loss_in[...], keepdims=True) * loss_scale
        loss_ref[...] = jnp.broadcast_to(total, loss_ref.shape)
    else:
        loss_ref[...] = loss


def text_shares(coeff_ref, left, image_refs):
    rows = image_refs[0].shape[0]
    part = None
    for r, image_ref in enumerate(image_refs):
        more = lax.dot_general(
            coeff_ref[r * rows : (r + 1) * rows, left : left + rows],
            image_ref[...],
            TN,
            preferred_element_type=jnp.float32,
        )
        part = more if part is None else part + more
    return part


def logit_terms(place, logit_scale, bias, images, texts, core=0, loss=None, loss_scale=None):
    rows, depth = images[0].shape
    height, count = len(images) * rows, len(texts) * rows
    coeff, loss_tile = shape_of(height, count, jnp.bfloat16), shape_of(8, PIECE, jnp.float32)
    shares = [shape_of(2 * rows, depth, jnp.bfloat16)] * 2 if core else []
    operands = (place, logit_scale, bias, *images, *texts) + ((loss,) if core else ())
    out_shape = [coeff, *shares, loss_tile]
    outs = pl.pallas_call(
        functools.partial(logit_kernel, core, loss_scale),
        out_shape=out_shape,
        in_specs=[SMEM, SMEM, SMEM] + [VMEM] * (len(operands) - 3),
        out_specs=[VMEM] * len(out_shape),
        compiler_params=pltpu.CompilerParams(vmem_limit_bytes=PAIR_VMEM),
        cost_estimate=cost((2 if core else 1) * height * count * depth),
        name="other_logits" if core else "own_logits",
    )(*operands)
    return outs[0], outs[1:-1], outs[-1]


def cost(multiplies):
    return pl.CostEstimate(flops=2 * multiplies, bytes_accessed=8 * 2**20, transcendentals=0)


def text_kernel(first, coeff_ref, came_ref, *refs):
    image_refs, outs = refs[:4], refs[4:]
    rows = outs[0].shape[0]
    for k in (1, 0):
        total = text_shares(coeff_ref, first + k * rows, image_refs) + decode(came_ref[k * rows : (k + 1) * rows, :])
        outs[k][...] = total if outs[k].dtype == jnp.float32 else encode(total)


def text_terms(first, dtype, coeff, came, images):
    rows, depth = images[0].shape
    return pl.pallas_call(
        functools.partial(text_kernel, first),
        out_shape=[shape_of(rows, depth, dtype)] * 2,
        in_specs=[VMEM] * 6,
        out_specs=[VMEM] * 2,
        compiler_params=pltpu.CompilerParams(vmem_limit_bytes=PAIR_VMEM),
        cost_estimate=cost(2 * rows * coeff.shape[0] * depth),
        name="text_terms",
    )(coeff, came, *images)


def image_kernel(first, own_ref, other_ref, *refs):
    text_refs, outs = refs[:8], refs[8:]
    rows = outs[0].shape[0]
    for k, out in enumerate(outs):
        top = first + k * rows
        total = None
        for t, text_ref in enumerate(text_refs):
            coeff_ref, left = (own_ref, other_ref)[t // 4], t % 4 * rows
            more = jnp.dot(
                coeff_ref[top : top + rows, left : left + rows], text_ref[...], preferred_element_type=jnp.float32
            )
            total = more if total is None else total + more
        out[...] = total if out.dtype == jnp.float32 else encode(total)


def image_terms(first, count, dtype, coeffs, texts):
    rows, depth = texts[0].shape
    return pl.pallas_call(
        functools.partial(image_kernel, first),
        out_shape=[shape_of(rows, depth, dtype)] * count,
        in_specs=[VMEM] * 10,
        out_specs=[VMEM] * count,
        compiler_params=pltpu.CompilerParams(vmem_limit_bytes=PAIR_VMEM),
        cost_estimate=cost(2 * count * rows * coeffs[0].shape[1] * depth),
        name="image_terms",
    )(*coeffs, *texts)


def small_call(kernel, name, out_shape, operands):
    return pl.pallas_call(
        kernel,
        out_shape=out_shape,
        in_specs=[VMEM] * len(operands),
        out_specs=[VMEM] * len(out_shape),
        compiler_params=pltpu.CompilerParams(vmem_limit_bytes=SMALL_VMEM),
        name=name,
    )(*operands)


def fold_kernel(own_ref, came_ref, kept, sent):
    sent[...] = encode(own_ref[PIECE:, :] + decode(came_ref[PIECE:, :]))
    kept[...] = own_ref[:PIECE, :] + decode(came_ref[:PIECE, :])


def fold(own, came):
    depth = own.shape[1]
    out_shape = [shape_of(PIECE, depth, jnp.float32), shape_of(PIECE, depth, jnp.bfloat16)]
    return small_call(fold_kernel, "fold", out_shape, (own, came))


def add_kernel(own_ref, came_ref, out_ref):
    out_ref[...] = encode(own_ref[...] + decode(came_ref[...]))


def add_codes(own, came):
    return small_call(add_kernel, "add_codes", [shape_of(*own.shape, jnp.bfloat16)], (own, came))[0]


def finish_kernel(raw_ref, own_ref, ring_ref, far_ref, loss_ref, loss_in, out_ref, loss_out):
    loss_out[0] = jnp.max(loss_ref[...] + loss_in[...])
    grad = own_ref[...] + decode(ring_ref[...]) + decode(far_ref[...])
    wide = raw_ref[...].astype(jnp.float32)
    inverse = lax.rsqrt(jnp.sum(wide * wide, axis=1, keepdims=True) + 1e-06)
    unit = wide * inverse
    out_ref[...] = inverse * (grad - unit * jnp.sum(unit * grad, axis=1, keepdims=True))


def finish(raw, own, ring, far, loss, loss_in):
    return pl.pallas_call(
        finish_kernel,
        out_shape=[shape_of(*raw.shape, jnp.float32), jax.ShapeDtypeStruct((1,), jnp.float32)],
        in_specs=[VMEM] * 6,
        out_specs=[VMEM, SMEM],
        compiler_params=pltpu.CompilerParams(vmem_limit_bytes=SMALL_VMEM),
        name="finish",
    )(raw, own, ring, far, loss, loss_in)


def gather(image, text):
    groups = ((image, IMAGE_PAIRS), (text, TEXT_PAIRS))
    far = [swap(unit, pairs["x"]) for unit, pairs in groups]
    *far, image, text = lax.optimization_barrier((*far, image, text))
    groups = ((image, IMAGE_PAIRS), (text, TEXT_PAIRS))
    far = [jnp.concatenate([part, swap(part, pairs["z"])], axis=0) for part, (_, pairs) in zip(far, groups)]
    near = [jnp.concatenate([unit, swap(unit, pairs["y"])], axis=0) for unit, pairs in groups]
    *far, near[0], near[1] = lax.optimization_barrier((*far, *near))
    far_late = [swap(part, pairs["y"]) for part, (_, pairs) in zip(far, groups)]
    near_late = [swap(part, pairs["z"]) for part, (_, pairs) in zip(near, groups)]
    images, texts = ([near[k], far[k], near_late[k], far_late[k]] for k in range(2))
    late_core = [after(far[1], *near_late, *far_late), *texts[2:]]
    return images, texts + [swap(part, CORE) for part in (near[1], *late_core)]


def after(value, *others):
    return lax.optimization_barrier((value, *others))[0]


def shards(images, texts, logit_scale, bias):
    place = (lax.axis_index("img") * lax.axis_size("txt") + lax.axis_index("txt")).astype(jnp.int32).reshape(1)
    image_all, text_all = gather(*unit_rows(images, texts))
    count = images.shape[0] * lax.axis_size("img") * lax.axis_size("txt")
    own_coeff, _, loss = logit_terms(place, logit_scale, bias, image_all, text_all[:4])
    other_coeff, other, loss = logit_terms(
        place, logit_scale, bias, image_all, text_all[4:], CORE, loss, 1.0 / count
    )
    coeffs = (own_coeff, other_coeff)

    other_late = swap(other[1], CORE)
    loss = loss + swap(loss, CORE)
    near_late, far_late = image_terms(4 * PIECE, 2, jnp.bfloat16, coeffs, text_all)
    image_far = swap(far_late, IMAGE_PAIRS["y"])
    image_near = swap(near_late, IMAGE_PAIRS["z"])
    text_near, text_far = text_terms(
        4 * PIECE, jnp.bfloat16, after(own_coeff, loss, near_late), other_late, image_all
    )
    text_far = swap(text_far, TEXT_PAIRS["y"])
    text_near = swap(text_near, TEXT_PAIRS["z"])
    other_early = swap(other[0], CORE)
    near_early, far_early = image_terms(0, 2, jnp.float32, (after(own_coeff, far_late), other_coeff), text_all)
    text_early = text_terms(0, jnp.float32, after(own_coeff, near_early), other_early, image_all)

    image_kept, image_sent = fold(far_early, image_far)
    image_far = swap(image_sent, IMAGE_PAIRS["z"])
    loss = after(loss, text_early[0])
    loss = loss + swap(loss, IMAGE_PAIRS["y"])
    text_kept, text_sent = fold(text_early[1], after(text_far, loss))
    text_far = swap(text_sent, TEXT_PAIRS["z"])
    image_own, image_sent = fold(near_early, image_near)
    image_near = swap(image_sent, IMAGE_PAIRS["y"])
    text_own, text_sent = fold(text_early[0], text_near)
    text_near = swap(text_sent, TEXT_PAIRS["y"])

    loss = after(loss, text_kept, image_own, text_own)
    loss = loss + swap(loss, IMAGE_PAIRS["x"])
    image_sent = add_codes(image_kept, after(image_far, loss))
    loss = loss + swap(loss, TEXT_PAIRS["x"])
    text_sent = add_codes(text_kept, after(text_far, loss))
    loss = after(loss, text_sent)
    for mask in (IMAGE_PAIRS["z"], TEXT_PAIRS["y"]):
        loss = loss + swap(loss, mask)
    last = swap(loss, TEXT_PAIRS["z"])
    image_grad, _ = finish(images, image_own, image_near, swap(image_sent, IMAGE_PAIRS["x"]), loss, loss)
    text_grad, loss = finish(texts, text_own, text_near, swap(text_sent, TEXT_PAIRS["x"]), loss, last)
    return loss, image_grad, text_grad


def solution(mesh):
    placed = (P(("img", "txt"), None), P(("txt", "img"), None), P(), P())
    return jax.shard_map(
        shards,
        mesh=mesh,
        in_specs=placed,
        out_specs=(P(), P(("img", "txt"), None), P(("txt", "img"), None)),
        check_vma=False,
    )
```

```python
import functools

import jax
import jax.numpy as jnp
from jax import lax
from jax.experimental import pallas as pl
from jax.experimental.pallas import tpu as pltpu
from jax.sharding import PartitionSpec as P

IMAGE_PAIRS = {"x": 2 << 3, "y": 1, "z": 4 << 3}
TEXT_PAIRS = {"x": (2 << 3) + 4, "y": 3, "z": 12 << 3}
CORE = 1 << 3
PIECE = 128
ROWS = ("", "y", "x", "xz", "z", "yz", "xy", "xyz")
PAIR_VMEM = 12 * 2**20
SMALL_VMEM = 8 * 2**20
LOG2E = 1.4426950408889634
LN2 = 0.6931471805599453
NT = (((1,), (1,)), ((), ()))
NN = (((1,), (0,)), ((), ()))
TN = (((0,), (0,)), ((), ()))
HBM = pl.BlockSpec(memory_space=pl.ANY)
SMEM = pl.BlockSpec(memory_space=pltpu.SMEM)
VMEM = pl.BlockSpec(memory_space=pltpu.VMEM)


def shape_of(rows, depth, dtype):
    return jax.ShapeDtypeStruct((rows, depth), dtype)


def swap(value, mask):
    axes = ("img", "txt")
    return lax.ppermute(value, axes, [(k ^ mask, k) for k in range(lax.axis_size(axes))])


def encode(value):
    square = value * value
    return ((square * value) * (square * square)).astype(jnp.bfloat16)


def decode(code):
    wide = code.astype(jnp.float32)
    root = jnp.exp2(jnp.log2(jnp.abs(wide)) * (1.0 / 7.0))
    return jnp.where(wide < 0.0, -root, root)


def unit_kernel(images_ref, texts_ref, image_out, text_out, raw, sems):
    loads = [pltpu.make_async_copy(ref, raw.at[k], sems.at[k]) for k, ref in enumerate((images_ref, texts_ref))]
    for load in loads:
        load.start()
    for k, out in enumerate((image_out, text_out)):
        loads[k].wait()
        wide = raw[k].astype(jnp.float32)
        inverse = lax.rsqrt(jnp.sum(wide * wide, axis=1, keepdims=True) + 1e-06)
        out[...] = (wide * inverse).astype(jnp.bfloat16)


def unit_rows(images, texts):
    out = shape_of(*images.shape, jnp.bfloat16)
    return pl.pallas_call(
        unit_kernel,
        out_shape=[out, out],
        in_specs=[HBM, HBM],
        out_specs=[VMEM, VMEM],
        scratch_shapes=[pltpu.VMEM((2, *images.shape), jnp.bfloat16), pltpu.SemaphoreType.DMA((2,))],
        compiler_params=pltpu.CompilerParams(vmem_limit_bytes=60 * 2**20),
        name="unit_rows",
    )(images, texts)


def row_masks(pairs):
    return [sum(pairs[axis] for axis in axes) for axes in ROWS]


ORDER = (2, 3, 0, 1)


def logit_kernel(core, loss_scale, place_ref, temper_ref, shift_ref, *refs):
    image_refs, text_refs = refs[:4], refs[4:8]
    if core:
        loss_in, coeff_ref, other_refs, loss_ref = refs[8], refs[9], refs[10:12], refs[12]
    else:
        coeff_ref, loss_ref = refs[8:]
    rows = image_refs[0].shape[0]
    pieces = rows // PIECE

    place = place_ref[0]
    image_base = [lax.bitwise_xor(place, mask) * PIECE for mask in row_masks(IMAGE_PAIRS)]
    text_base = []
    for mask in row_masks(TEXT_PAIRS):
        flat = lax.bitwise_xor(place, mask ^ core)
        text_base.append((lax.rem(flat, 8) * 16 + lax.div(flat, 8)) * PIECE)

    temper = jnp.broadcast_to(temper_ref[...], (1, PIECE))
    slope = temper * LOG2E
    shift = jnp.broadcast_to(shift_ref[...], (1, PIECE))
    apart = lax.broadcasted_iota(jnp.int32, (PIECE, PIECE), 0) - lax.broadcasted_iota(
        jnp.int32, (PIECE, PIECE), 1
    )
    quarter = PIECE // 4
    loss_sum = jnp.zeros((8, PIECE), jnp.float32)
    own_sum = jnp.zeros((8, PIECE), jnp.float32)
    def put_shares(t):
        other_refs[t // 2][t % 2 * rows : (t % 2 + 1) * rows, :] = encode(
            text_shares(coeff_ref, t * rows, image_refs)
        )

    for n, t in enumerate(ORDER):
        left = t * rows
        for r, image_ref in enumerate(image_refs):
            dots = lax.dot_general(image_ref[...], text_refs[t][...], NT, preferred_element_type=jnp.float32)
            for a in range(pieces):
                top = r * rows + a * PIECE
                for b in range(pieces):
                    power = dots[a * PIECE : (a + 1) * PIECE, b * PIECE : (b + 1) * PIECE] * slope + shift
                    grown = jnp.exp2(power)
                    match = apart == text_base[t * pieces + b] - image_base[r * pieces + a]
                    weight = jnp.where(match, -1.0, grown) * pl.reciprocal(1.0 + grown) * temper
                    column = left + b * PIECE
                    coeff_ref[top : top + PIECE, column : column + PIECE] = weight.astype(jnp.bfloat16)
                    g = [grown[k * quarter : (k + 1) * quarter] for k in range(4)]
                    low = g[0] + g[1] + g[0] * g[1]
                    high = g[2] + g[3] + g[2] * g[3]
                    terms = jnp.log(1.0 + (low + high + low * high))
                    chosen = jnp.where(match, power, 0.0)
                    for k in range(quarter // 8):
                        loss_sum = loss_sum + terms[k * 8 : (k + 1) * 8]
                    for k in range(PIECE // 8):
                        own_sum = own_sum + chosen[k * 8 : (k + 1) * 8]
        if core and n:
            put_shares(ORDER[n - 1])
    if core:
        put_shares(ORDER[-1])
    loss = loss_sum - LN2 * own_sum
    if core:
        total = jnp.sum(loss + loss_in[...], keepdims=True) * loss_scale
        loss_ref[...] = jnp.broadcast_to(total, loss_ref.shape)
    else:
        loss_ref[...] = loss


def text_shares(coeff_ref, left, image_refs):
    rows = image_refs[0].shape[0]
    part = None
    for r, image_ref in enumerate(image_refs):
        more = lax.dot_general(
            coeff_ref[r * rows : (r + 1) * rows, left : left + rows],
            image_ref[...],
            TN,
            preferred_element_type=jnp.float32,
        )
        part = more if part is None else part + more
    return part


def logit_terms(scalars, images, texts, core=0, loss=None, loss_scale=None):
    rows, depth = images[0].shape
    height, count = len(images) * rows, len(texts) * rows
    coeff, loss_tile = shape_of(height, count, jnp.bfloat16), shape_of(8, PIECE, jnp.float32)
    shares = [shape_of(2 * rows, depth, jnp.bfloat16)] * 2 if core else []
    operands = (*scalars, *images, *texts) + ((loss,) if core else ())
    out_shape = [coeff, *shares, loss_tile]
    outs = pl.pallas_call(
        functools.partial(logit_kernel, core, loss_scale),
        out_shape=out_shape,
        in_specs=[SMEM] + [VMEM] * (len(operands) - 1),
        out_specs=[VMEM] * len(out_shape),
        compiler_params=pltpu.CompilerParams(vmem_limit_bytes=PAIR_VMEM),
        cost_estimate=cost((2 if core else 1) * height * count * depth),
        name="other_logits" if core else "own_logits",
    )(*operands)
    return outs[0], outs[1:-1], outs[-1]


def cost(multiplies):
    return pl.CostEstimate(flops=2 * multiplies, bytes_accessed=8 * 2**20, transcendentals=0)


def text_kernel(first, coeff_ref, came_ref, *refs):
    image_refs, outs = refs[:4], refs[4:]
    rows = outs[0].shape[0]
    for k in (1, 0):
        total = text_shares(coeff_ref, first + k * rows, image_refs) + decode(came_ref[k * rows : (k + 1) * rows, :])
        outs[k][...] = total if outs[k].dtype == jnp.float32 else encode(total)


def text_terms(first, dtype, coeff, came, images):
    rows, depth = images[0].shape
    return pl.pallas_call(
        functools.partial(text_kernel, first),
        out_shape=[shape_of(rows, depth, dtype)] * 2,
        in_specs=[VMEM] * 6,
        out_specs=[VMEM] * 2,
        compiler_params=pltpu.CompilerParams(vmem_limit_bytes=PAIR_VMEM),
        cost_estimate=cost(2 * rows * coeff.shape[0] * depth),
        name="text_terms",
    )(coeff, came, *images)


def image_kernel(first, own_ref, other_ref, *refs):
    text_refs, outs = refs[:8], refs[8:]
    rows = outs[0].shape[0]
    for k, out in enumerate(outs):
        top = first + k * rows
        total = None
        for t, text_ref in enumerate(text_refs):
            coeff_ref, left = (own_ref, other_ref)[t // 4], t % 4 * rows
            more = jnp.dot(
                coeff_ref[top : top + rows, left : left + rows], text_ref[...], preferred_element_type=jnp.float32
            )
            total = more if total is None else total + more
        out[...] = total if out.dtype == jnp.float32 else encode(total)


def image_terms(first, count, dtype, coeffs, texts):
    rows, depth = texts[0].shape
    return pl.pallas_call(
        functools.partial(image_kernel, first),
        out_shape=[shape_of(rows, depth, dtype)] * count,
        in_specs=[VMEM] * 10,
        out_specs=[VMEM] * count,
        compiler_params=pltpu.CompilerParams(vmem_limit_bytes=PAIR_VMEM),
        cost_estimate=cost(2 * count * rows * coeffs[0].shape[1] * depth),
        name="image_terms",
    )(*coeffs, *texts)


def small_call(kernel, name, out_shape, operands):
    return pl.pallas_call(
        kernel,
        out_shape=out_shape,
        in_specs=[VMEM] * len(operands),
        out_specs=[VMEM] * len(out_shape),
        compiler_params=pltpu.CompilerParams(vmem_limit_bytes=SMALL_VMEM),
        name=name,
    )(*operands)


def fold_kernel(own_ref, came_ref, kept, sent):
    sent[...] = encode(own_ref[PIECE:, :] + decode(came_ref[PIECE:, :]))
    kept[...] = own_ref[:PIECE, :] + decode(came_ref[:PIECE, :])


def fold(own, came):
    depth = own.shape[1]
    out_shape = [shape_of(PIECE, depth, jnp.float32), shape_of(PIECE, depth, jnp.bfloat16)]
    return small_call(fold_kernel, "fold", out_shape, (own, came))


def add_kernel(own_ref, came_ref, out_ref):
    out_ref[...] = encode(own_ref[...] + decode(came_ref[...]))


def add_codes(own, came):
    return small_call(add_kernel, "add_codes", [shape_of(*own.shape, jnp.bfloat16)], (own, came))[0]


def finish_kernel(raw_ref, own_ref, ring_ref, far_ref, loss_ref, loss_in, out_ref, loss_out):
    loss_out[0] = jnp.max(loss_ref[...] + loss_in[...])
    grad = own_ref[...] + decode(ring_ref[...]) + decode(far_ref[...])
    wide = raw_ref[...].astype(jnp.float32)
    inverse = lax.rsqrt(jnp.sum(wide * wide, axis=1, keepdims=True) + 1e-06)
    unit = wide * inverse
    out_ref[...] = inverse * (grad - unit * jnp.sum(unit * grad, axis=1, keepdims=True))


def finish(raw, own, ring, far, loss, loss_in):
    return pl.pallas_call(
        finish_kernel,
        out_shape=[shape_of(*raw.shape, jnp.float32), jax.ShapeDtypeStruct((1,), jnp.float32)],
        in_specs=[VMEM] * 6,
        out_specs=[VMEM, SMEM],
        compiler_params=pltpu.CompilerParams(vmem_limit_bytes=SMALL_VMEM),
        name="finish",
    )(raw, own, ring, far, loss, loss_in)


def gather(image, text, scalars):
    groups = ((image, IMAGE_PAIRS), (text, TEXT_PAIRS))
    far = [swap(unit, pairs["x"]) for unit, pairs in groups]
    *far, image, text, scalars = lax.optimization_barrier((*far, image, text, scalars))
    groups = ((image, IMAGE_PAIRS), (text, TEXT_PAIRS))
    far = [jnp.concatenate([part, swap(part, pairs["z"])], axis=0) for part, (_, pairs) in zip(far, groups)]
    near = [jnp.concatenate([unit, swap(unit, pairs["y"])], axis=0) for unit, pairs in groups]
    *far, near[0], near[1] = lax.optimization_barrier((*far, *near))
    far_late = [swap(part, pairs["y"]) for part, (_, pairs) in zip(far, groups)]
    near_late = [swap(part, pairs["z"]) for part, (_, pairs) in zip(near, groups)]
    images, texts = ([near[k], far[k], near_late[k], far_late[k]] for k in range(2))
    late_core = [after(far[1], *near_late, *far_late), *texts[2:]]
    return images, texts + [swap(part, CORE) for part in (near[1], *late_core)], scalars


def after(value, *others):
    return lax.optimization_barrier((value, *others))[0]


def shards(images, texts, logit_scale, bias):
    place = (lax.axis_index("img") * lax.axis_size("txt") + lax.axis_index("txt")).astype(jnp.int32).reshape(1)
    scalars = (place, jnp.exp(logit_scale).reshape(1, 1), (bias * LOG2E).reshape(1, 1))
    image_all, text_all, scalars = gather(*unit_rows(images, texts), scalars)
    count = images.shape[0] * lax.axis_size("img") * lax.axis_size("txt")
    own_coeff, _, loss = logit_terms(scalars, image_all, text_all[:4])
    other_coeff, other, loss = logit_terms(scalars, image_all, text_all[4:], CORE, loss, 1.0 / count)
    coeffs = (own_coeff, other_coeff)

    other_late = swap(other[1], CORE)
    other_early = swap(other[0], CORE)
    loss = loss + swap(loss, CORE)
    near_late, far_late = image_terms(4 * PIECE, 2, jnp.bfloat16, coeffs, text_all)
    image_far = swap(far_late, IMAGE_PAIRS["y"])
    image_near = swap(near_late, IMAGE_PAIRS["z"])
    text_near, text_far = text_terms(
        4 * PIECE, jnp.bfloat16, after(own_coeff, loss, near_late, other_early), other_late, image_all
    )
    text_far = swap(text_far, TEXT_PAIRS["y"])
    text_near = swap(text_near, TEXT_PAIRS["z"])
    tiles = swap(jnp.broadcast_to(loss[None], (64, *loss.shape)), IMAGE_PAIRS["x"])
    near_early, far_early = image_terms(0, 2, jnp.float32, (after(own_coeff, far_late), other_coeff), text_all)
    text_early = text_terms(0, jnp.float32, after(own_coeff, near_early), other_early, image_all)

    image_kept, image_sent = fold(far_early, image_far)
    image_far = swap(image_sent, IMAGE_PAIRS["z"])
    loss = after(loss, text_early[0]) + tiles[0]
    loss = loss + swap(loss, IMAGE_PAIRS["y"])
    text_kept, text_sent = fold(text_early[1], after(text_far, loss))
    text_far = swap(text_sent, TEXT_PAIRS["z"])
    image_own, image_sent = fold(near_early, image_near)
    image_near = swap(image_sent, IMAGE_PAIRS["y"])
    text_own, text_sent = fold(text_early[0], text_near)
    text_near = swap(text_sent, TEXT_PAIRS["y"])

    loss = after(loss, text_kept)
    loss = loss + swap(loss, TEXT_PAIRS["x"])
    image_sent = add_codes(image_kept, image_far)
    loss = loss + swap(loss, IMAGE_PAIRS["z"])
    text_sent = add_codes(text_kept, after(text_far, loss))
    loss = loss + swap(after(loss, text_sent), TEXT_PAIRS["y"])
    last = swap(loss, TEXT_PAIRS["z"])
    image_grad, _ = finish(images, image_own, image_near, swap(image_sent, IMAGE_PAIRS["x"]), loss, loss)
    text_grad, loss = finish(texts, text_own, text_near, swap(text_sent, TEXT_PAIRS["x"]), loss, last)
    return loss, image_grad, text_grad


def solution(mesh):
    placed = (P(("img", "txt"), None), P(("txt", "img"), None), P(), P())
    return jax.shard_map(
        shards,
        mesh=mesh,
        in_specs=placed,
        out_specs=(P(), P(("img", "txt"), None), P(("txt", "img"), None)),
        check_vma=False,
    )
```

```python
import functools

import jax
import jax.numpy as jnp
from jax import lax
from jax.experimental import pallas as pl
from jax.experimental.pallas import tpu as pltpu
from jax.sharding import PartitionSpec as P

IMAGE_PAIRS = {"x": 2 << 3, "y": 1, "z": 4 << 3}
TEXT_PAIRS = {"x": (2 << 3) + 4, "y": 3, "z": 12 << 3}
CORE = 1 << 3
PIECE = 128
ROWS = ("", "y", "x", "xz", "z", "yz", "xy", "xyz")
PAIR_VMEM = 12 * 2**20
SMALL_VMEM = 8 * 2**20
LOG2E = 1.4426950408889634
LN2 = 0.6931471805599453
NT = (((1,), (1,)), ((), ()))
NN = (((1,), (0,)), ((), ()))
TN = (((0,), (0,)), ((), ()))
HBM = pl.BlockSpec(memory_space=pl.ANY)
SMEM = pl.BlockSpec(memory_space=pltpu.SMEM)
VMEM = pl.BlockSpec(memory_space=pltpu.VMEM)


def shape_of(rows, depth, dtype):
    return jax.ShapeDtypeStruct((rows, depth), dtype)


def swap(value, mask):
    axes = ("img", "txt")
    return lax.ppermute(value, axes, [(k ^ mask, k) for k in range(lax.axis_size(axes))])


def encode(value):
    square = value * value
    return ((square * value) * (square * square)).astype(jnp.bfloat16)


def decode(code):
    wide = code.astype(jnp.float32)
    root = jnp.exp2(jnp.log2(jnp.abs(wide)) * (1.0 / 7.0))
    return jnp.where(wide < 0.0, -root, root)


def unit_kernel(images_ref, texts_ref, image_out, text_out, raw, sems):
    loads = [pltpu.make_async_copy(ref, raw.at[k], sems.at[k]) for k, ref in enumerate((images_ref, texts_ref))]
    for load in loads:
        load.start()
    for k, out in enumerate((image_out, text_out)):
        loads[k].wait()
        wide = raw[k].astype(jnp.float32)
        inverse = lax.rsqrt(jnp.sum(wide * wide, axis=1, keepdims=True) + 1e-06)
        out[...] = (wide * inverse).astype(jnp.bfloat16)


def unit_rows(images, texts):
    out = shape_of(*images.shape, jnp.bfloat16)
    return pl.pallas_call(
        unit_kernel,
        out_shape=[out, out],
        in_specs=[HBM, HBM],
        out_specs=[VMEM, VMEM],
        scratch_shapes=[pltpu.VMEM((2, *images.shape), jnp.bfloat16), pltpu.SemaphoreType.DMA((2,))],
        compiler_params=pltpu.CompilerParams(vmem_limit_bytes=60 * 2**20),
        name="unit_rows",
    )(images, texts)


def far_kernel(images_ref, texts_ref, *out_refs):
    for raw_ref, out_ref in zip((images_ref, texts_ref), out_refs):
        wide = raw_ref[...].astype(jnp.float32)
        inverse = lax.rsqrt(jnp.sum(wide * wide, axis=1, keepdims=True) + 1e-06)
        out_ref[...] = (wide * inverse).astype(jnp.bfloat16)


def row_masks(pairs):
    return [sum(pairs[axis] for axis in axes) for axes in ROWS]


ORDER = (2, 3, 0, 1)


def logit_kernel(core, loss_scale, place_ref, temper_ref, shift_ref, *refs):
    image_refs, text_refs = refs[:4], refs[4:8]
    if core:
        loss_in, coeff_ref, other_refs, loss_ref = refs[8], refs[9], refs[10:12], refs[12]
    else:
        coeff_ref, loss_ref = refs[8:]
    rows = image_refs[0].shape[0]
    pieces = rows // PIECE

    place = place_ref[0]
    image_base = [lax.bitwise_xor(place, mask) * PIECE for mask in row_masks(IMAGE_PAIRS)]
    text_base = []
    for mask in row_masks(TEXT_PAIRS):
        flat = lax.bitwise_xor(place, mask ^ core)
        text_base.append((lax.rem(flat, 8) * 16 + lax.div(flat, 8)) * PIECE)

    temper = jnp.broadcast_to(temper_ref[...], (1, PIECE))
    slope = temper * LOG2E
    shift = jnp.broadcast_to(shift_ref[...], (1, PIECE))
    apart = lax.broadcasted_iota(jnp.int32, (PIECE, PIECE), 0) - lax.broadcasted_iota(
        jnp.int32, (PIECE, PIECE), 1
    )
    quarter = PIECE // 4
    loss_sum = jnp.zeros((8, PIECE), jnp.float32)
    own_sum = jnp.zeros((8, PIECE), jnp.float32)
    def put_shares(t):
        other_refs[t // 2][t % 2 * rows : (t % 2 + 1) * rows, :] = encode(
            text_shares(coeff_ref, t * rows, image_refs)
        )

    for n, t in enumerate(ORDER):
        left = t * rows
        for r, image_ref in enumerate(image_refs):
            dots = lax.dot_general(image_ref[...], text_refs[t][...], NT, preferred_element_type=jnp.float32)
            for a in range(pieces):
                top = r * rows + a * PIECE
                for b in range(pieces):
                    power = dots[a * PIECE : (a + 1) * PIECE, b * PIECE : (b + 1) * PIECE] * slope + shift
                    grown = jnp.exp2(power)
                    match = apart == text_base[t * pieces + b] - image_base[r * pieces + a]
                    weight = jnp.where(match, -1.0, grown) * pl.reciprocal(1.0 + grown) * temper
                    column = left + b * PIECE
                    coeff_ref[top : top + PIECE, column : column + PIECE] = weight.astype(jnp.bfloat16)
                    g = [grown[k * quarter : (k + 1) * quarter] for k in range(4)]
                    low = g[0] + g[1] + g[0] * g[1]
                    high = g[2] + g[3] + g[2] * g[3]
                    terms = jnp.log(1.0 + (low + high + low * high))
                    chosen = jnp.where(match, power, 0.0)
                    for k in range(quarter // 8):
                        loss_sum = loss_sum + terms[k * 8 : (k + 1) * 8]
                    for k in range(PIECE // 8):
                        own_sum = own_sum + chosen[k * 8 : (k + 1) * 8]
        if core and n:
            put_shares(ORDER[n - 1])
    if core:
        put_shares(ORDER[-1])
    loss = loss_sum - LN2 * own_sum
    if core:
        total = jnp.sum(loss + loss_in[...], keepdims=True) * loss_scale
        loss_ref[...] = jnp.broadcast_to(total, loss_ref.shape)
    else:
        loss_ref[...] = loss


def text_shares(coeff_ref, left, image_refs):
    rows = image_refs[0].shape[0]
    part = None
    for r, image_ref in enumerate(image_refs):
        more = lax.dot_general(
            coeff_ref[r * rows : (r + 1) * rows, left : left + rows],
            image_ref[...],
            TN,
            preferred_element_type=jnp.float32,
        )
        part = more if part is None else part + more
    return part


def logit_terms(scalars, images, texts, core=0, loss=None, loss_scale=None):
    rows, depth = images[0].shape
    height, count = len(images) * rows, len(texts) * rows
    coeff, loss_tile = shape_of(height, count, jnp.bfloat16), shape_of(8, PIECE, jnp.float32)
    shares = [shape_of(2 * rows, depth, jnp.bfloat16)] * 2 if core else []
    operands = (*scalars, *images, *texts) + ((loss,) if core else ())
    out_shape = [coeff, *shares, loss_tile]
    outs = pl.pallas_call(
        functools.partial(logit_kernel, core, loss_scale),
        out_shape=out_shape,
        in_specs=[SMEM] + [VMEM] * (len(operands) - 1),
        out_specs=[VMEM] * len(out_shape),
        compiler_params=pltpu.CompilerParams(vmem_limit_bytes=PAIR_VMEM),
        cost_estimate=cost((2 if core else 1) * height * count * depth),
        name="other_logits" if core else "own_logits",
    )(*operands)
    return outs[0], outs[1:-1], outs[-1]


def cost(multiplies):
    return pl.CostEstimate(flops=2 * multiplies, bytes_accessed=8 * 2**20, transcendentals=0)


def text_kernel(first, coeff_ref, came_ref, *refs):
    image_refs, outs = refs[:4], refs[4:]
    rows = outs[0].shape[0]
    for k in (1, 0):
        total = text_shares(coeff_ref, first + k * rows, image_refs) + decode(came_ref[k * rows : (k + 1) * rows, :])
        outs[k][...] = total if outs[k].dtype == jnp.float32 else encode(total)


def text_terms(first, dtype, coeff, came, images):
    rows, depth = images[0].shape
    return pl.pallas_call(
        functools.partial(text_kernel, first),
        out_shape=[shape_of(rows, depth, dtype)] * 2,
        in_specs=[VMEM] * 6,
        out_specs=[VMEM] * 2,
        compiler_params=pltpu.CompilerParams(vmem_limit_bytes=PAIR_VMEM),
        cost_estimate=cost(2 * rows * coeff.shape[0] * depth),
        name="text_terms",
    )(coeff, came, *images)


def image_kernel(first, own_ref, other_ref, *refs):
    text_refs, outs = refs[:8], refs[8:]
    rows = outs[0].shape[0]
    for k, out in enumerate(outs):
        top = first + k * rows
        total = None
        for t, text_ref in enumerate(text_refs):
            coeff_ref, left = (own_ref, other_ref)[t // 4], t % 4 * rows
            more = jnp.dot(
                coeff_ref[top : top + rows, left : left + rows], text_ref[...], preferred_element_type=jnp.float32
            )
            total = more if total is None else total + more
        out[...] = total if out.dtype == jnp.float32 else encode(total)


def image_terms(first, count, dtype, coeffs, texts):
    rows, depth = texts[0].shape
    return pl.pallas_call(
        functools.partial(image_kernel, first),
        out_shape=[shape_of(rows, depth, dtype)] * count,
        in_specs=[VMEM] * 10,
        out_specs=[VMEM] * count,
        compiler_params=pltpu.CompilerParams(vmem_limit_bytes=PAIR_VMEM),
        cost_estimate=cost(2 * count * rows * coeffs[0].shape[1] * depth),
        name="image_terms",
    )(*coeffs, *texts)


def small_call(kernel, name, out_shape, operands):
    return pl.pallas_call(
        kernel,
        out_shape=out_shape,
        in_specs=[VMEM] * len(operands),
        out_specs=[VMEM] * len(out_shape),
        compiler_params=pltpu.CompilerParams(vmem_limit_bytes=SMALL_VMEM),
        name=name,
    )(*operands)


def fold_kernel(own_ref, came_ref, kept, sent):
    sent[...] = encode(own_ref[PIECE:, :] + decode(came_ref[PIECE:, :]))
    kept[...] = own_ref[:PIECE, :] + decode(came_ref[:PIECE, :])


def fold(own, came):
    depth = own.shape[1]
    out_shape = [shape_of(PIECE, depth, jnp.float32), shape_of(PIECE, depth, jnp.bfloat16)]
    return small_call(fold_kernel, "fold", out_shape, (own, came))


def add_kernel(own_ref, came_ref, out_ref):
    out_ref[...] = encode(own_ref[...] + decode(came_ref[...]))


def add_codes(own, came):
    return small_call(add_kernel, "add_codes", [shape_of(*own.shape, jnp.bfloat16)], (own, came))[0]


def finish_kernel(raw_ref, own_ref, ring_ref, far_ref, loss_ref, loss_in, out_ref, loss_out):
    loss_out[0] = jnp.max(loss_ref[...] + loss_in[...])
    grad = own_ref[...] + decode(ring_ref[...]) + decode(far_ref[...])
    wide = raw_ref[...].astype(jnp.float32)
    inverse = lax.rsqrt(jnp.sum(wide * wide, axis=1, keepdims=True) + 1e-06)
    unit = wide * inverse
    out_ref[...] = inverse * (grad - unit * jnp.sum(unit * grad, axis=1, keepdims=True))


def finish(raw, own, ring, far, loss, loss_in):
    return pl.pallas_call(
        finish_kernel,
        out_shape=[shape_of(*raw.shape, jnp.float32), jax.ShapeDtypeStruct((1,), jnp.float32)],
        in_specs=[VMEM] * 6,
        out_specs=[VMEM, SMEM],
        compiler_params=pltpu.CompilerParams(vmem_limit_bytes=SMALL_VMEM),
        name="finish",
    )(raw, own, ring, far, loss, loss_in)


def gather(image, text, scalars):
    groups = ((image, IMAGE_PAIRS), (text, TEXT_PAIRS))
    far = [swap(raw, pairs["x"]) for raw, pairs in groups]
    image, text = unit_rows(image, text)
    *far, image, text, scalars = lax.optimization_barrier((*far, image, text, scalars))
    far = small_call(far_kernel, "far_units", [shape_of(*part.shape, part.dtype) for part in far], far)
    groups = ((image, IMAGE_PAIRS), (text, TEXT_PAIRS))
    far = [jnp.concatenate([part, swap(part, pairs["z"])], axis=0) for part, (_, pairs) in zip(far, groups)]
    near = [jnp.concatenate([unit, swap(unit, pairs["y"])], axis=0) for unit, pairs in groups]
    *far, near[0], near[1] = lax.optimization_barrier((*far, *near))
    far_late = [swap(part, pairs["y"]) for part, (_, pairs) in zip(far, groups)]
    near_late = [swap(part, pairs["z"]) for part, (_, pairs) in zip(near, groups)]
    images, texts = ([near[k], far[k], near_late[k], far_late[k]] for k in range(2))
    late_core = [after(far[1], *near_late, *far_late), *texts[2:]]
    return images, texts + [swap(part, CORE) for part in (near[1], *late_core)], scalars


def after(value, *others):
    return lax.optimization_barrier((value, *others))[0]


def shards(images, texts, logit_scale, bias):
    place = (lax.axis_index("img") * lax.axis_size("txt") + lax.axis_index("txt")).astype(jnp.int32).reshape(1)
    scalars = (place, jnp.exp(logit_scale).reshape(1, 1), (bias * LOG2E).reshape(1, 1))
    image_all, text_all, scalars = gather(images, texts, scalars)
    count = images.shape[0] * lax.axis_size("img") * lax.axis_size("txt")
    own_coeff, _, loss = logit_terms(scalars, image_all, text_all[:4])
    other_coeff, other, loss = logit_terms(scalars, image_all, text_all[4:], CORE, loss, 1.0 / count)
    coeffs = (own_coeff, other_coeff)

    other_late = swap(other[1], CORE)
    other_early = swap(other[0], CORE)
    loss = loss + swap(loss, CORE)
    near_late, far_late = image_terms(4 * PIECE, 2, jnp.bfloat16, coeffs, text_all)
    image_far = swap(far_late, IMAGE_PAIRS["y"])
    image_near = swap(near_late, IMAGE_PAIRS["z"])
    text_near, text_far = text_terms(
        4 * PIECE, jnp.bfloat16, after(own_coeff, loss, near_late, other_early), other_late, image_all
    )
    text_far = swap(text_far, TEXT_PAIRS["y"])
    text_near = swap(text_near, TEXT_PAIRS["z"])
    loss = after(loss, near_late)
    tiles = swap(jnp.broadcast_to(loss[None], (32, *loss.shape)), IMAGE_PAIRS["x"])
    loss = loss + tiles[0]
    near_early, far_early = image_terms(0, 2, jnp.float32, (after(own_coeff, far_late, loss), other_coeff), text_all)
    tiles = swap(jnp.broadcast_to(loss[None], (32, *loss.shape)), TEXT_PAIRS["x"])
    text_early = text_terms(0, jnp.float32, after(own_coeff, near_early), other_early, image_all)

    image_kept, image_sent = fold(far_early, image_far)
    image_far = swap(image_sent, IMAGE_PAIRS["z"])
    loss = after(loss, text_early[0]) + tiles[0]
    loss = loss + swap(loss, IMAGE_PAIRS["y"])
    text_kept, text_sent = fold(text_early[1], after(text_far, loss))
    text_far = swap(text_sent, TEXT_PAIRS["z"])
    image_own, image_sent = fold(near_early, image_near)
    image_near = swap(image_sent, IMAGE_PAIRS["y"])
    text_own, text_sent = fold(text_early[0], text_near)
    text_near = swap(text_sent, TEXT_PAIRS["y"])

    image_sent = add_codes(image_kept, image_far)
    loss = after(loss, text_kept)
    loss = loss + swap(loss, IMAGE_PAIRS["z"])
    loss = loss + swap(loss, TEXT_PAIRS["y"])
    text_sent = add_codes(text_kept, after(text_far, loss))
    last = swap(loss, TEXT_PAIRS["z"])
    image_grad, _ = finish(images, image_own, image_near, swap(image_sent, IMAGE_PAIRS["x"]), loss, loss)
    text_grad, loss = finish(texts, text_own, text_near, swap(text_sent, TEXT_PAIRS["x"]), loss, last)
    return loss, image_grad, text_grad


def solution(mesh):
    placed = (P(("img", "txt"), None), P(("txt", "img"), None), P(), P())
    return jax.shard_map(
        shards,
        mesh=mesh,
        in_specs=placed,
        out_specs=(P(), P(("img", "txt"), None), P(("txt", "img"), None)),
        check_vma=False,
    )
```

```python
import functools

import jax
import jax.numpy as jnp
from jax import lax
from jax.experimental import pallas as pl
from jax.experimental.pallas import tpu as pltpu
from jax.sharding import PartitionSpec as P

IMAGE_PAIRS = {"x": 2 << 3, "y": 1, "z": 4 << 3}
TEXT_PAIRS = {"x": (2 << 3) + 4, "y": 3, "z": 12 << 3}
CORE = 1 << 3
PIECE = 128
ROWS = ("", "y", "x", "xz", "z", "yz", "xy", "xyz")
PAIR_VMEM = 12 * 2**20
SMALL_VMEM = 8 * 2**20
LOG2E = 1.4426950408889634
LN2 = 0.6931471805599453
NT = (((1,), (1,)), ((), ()))
NN = (((1,), (0,)), ((), ()))
TN = (((0,), (0,)), ((), ()))
HBM = pl.BlockSpec(memory_space=pl.ANY)
SMEM = pl.BlockSpec(memory_space=pltpu.SMEM)
VMEM = pl.BlockSpec(memory_space=pltpu.VMEM)


def shape_of(rows, depth, dtype):
    return jax.ShapeDtypeStruct((rows, depth), dtype)


def swap(value, mask):
    axes = ("img", "txt")
    return lax.ppermute(value, axes, [(k ^ mask, k) for k in range(lax.axis_size(axes))])


def encode(value):
    square = value * value
    return ((square * value) * (square * square)).astype(jnp.bfloat16)


def decode(code):
    wide = code.astype(jnp.float32)
    root = jnp.exp2(jnp.log2(jnp.abs(wide)) * (1.0 / 7.0))
    return jnp.where(wide < 0.0, -root, root)


def unit_kernel(images_ref, texts_ref, image_out, text_out, raw, sems):
    loads = [pltpu.make_async_copy(ref, raw.at[k], sems.at[k]) for k, ref in enumerate((images_ref, texts_ref))]
    for load in loads:
        load.start()
    for k, out in enumerate((image_out, text_out)):
        loads[k].wait()
        wide = raw[k].astype(jnp.float32)
        inverse = lax.rsqrt(jnp.sum(wide * wide, axis=1, keepdims=True) + 1e-06)
        out[...] = (wide * inverse).astype(jnp.bfloat16)


def unit_rows(images, texts):
    out = shape_of(*images.shape, jnp.bfloat16)
    return pl.pallas_call(
        unit_kernel,
        out_shape=[out, out],
        in_specs=[HBM, HBM],
        out_specs=[VMEM, VMEM],
        scratch_shapes=[pltpu.VMEM((2, *images.shape), jnp.bfloat16), pltpu.SemaphoreType.DMA((2,))],
        compiler_params=pltpu.CompilerParams(vmem_limit_bytes=60 * 2**20),
        name="unit_rows",
    )(images, texts)


def far_kernel(images_ref, texts_ref, *out_refs):
    for raw_ref, out_ref in zip((images_ref, texts_ref), out_refs):
        wide = raw_ref[...].astype(jnp.float32)
        inverse = lax.rsqrt(jnp.sum(wide * wide, axis=1, keepdims=True) + 1e-06)
        out_ref[...] = (wide * inverse).astype(jnp.bfloat16)


def row_masks(pairs):
    return [sum(pairs[axis] for axis in axes) for axes in ROWS]


ORDER = (2, 3, 0, 1)


def logit_kernel(core, loss_scale, place_ref, temper_ref, shift_ref, *refs):
    image_refs, text_refs = refs[:4], refs[4:8]
    if core:
        loss_in, coeff_ref, other_refs, loss_ref = refs[8], refs[9], refs[10:12], refs[12]
    else:
        coeff_ref, loss_ref = refs[8:]
    rows = image_refs[0].shape[0]
    pieces = rows // PIECE

    place = place_ref[0]
    image_base = [lax.bitwise_xor(place, mask) * PIECE for mask in row_masks(IMAGE_PAIRS)]
    text_base = []
    for mask in row_masks(TEXT_PAIRS):
        flat = lax.bitwise_xor(place, mask ^ core)
        text_base.append((lax.rem(flat, 8) * 16 + lax.div(flat, 8)) * PIECE)

    temper = jnp.broadcast_to(temper_ref[...], (1, PIECE))
    slope = temper * LOG2E
    shift = jnp.broadcast_to(shift_ref[...], (1, PIECE))
    apart = lax.broadcasted_iota(jnp.int32, (PIECE, PIECE), 0) - lax.broadcasted_iota(
        jnp.int32, (PIECE, PIECE), 1
    )
    quarter = PIECE // 4
    loss_sum = jnp.zeros((8, PIECE), jnp.float32)
    own_sum = jnp.zeros((8, PIECE), jnp.float32)
    def put_shares(t):
        other_refs[t // 2][t % 2 * rows : (t % 2 + 1) * rows, :] = encode(
            text_shares(coeff_ref, t * rows, image_refs)
        )

    for n, t in enumerate(ORDER):
        left = t * rows
        for r, image_ref in enumerate(image_refs):
            dots = lax.dot_general(image_ref[...], text_refs[t][...], NT, preferred_element_type=jnp.float32)
            for a in range(pieces):
                top = r * rows + a * PIECE
                for b in range(pieces):
                    power = dots[a * PIECE : (a + 1) * PIECE, b * PIECE : (b + 1) * PIECE] * slope + shift
                    grown = jnp.exp2(power)
                    match = apart == text_base[t * pieces + b] - image_base[r * pieces + a]
                    weight = jnp.where(match, -1.0, grown) * pl.reciprocal(1.0 + grown) * temper
                    column = left + b * PIECE
                    coeff_ref[top : top + PIECE, column : column + PIECE] = weight.astype(jnp.bfloat16)
                    g = [grown[k * quarter : (k + 1) * quarter] for k in range(4)]
                    low = g[0] + g[1] + g[0] * g[1]
                    high = g[2] + g[3] + g[2] * g[3]
                    terms = jnp.log(1.0 + (low + high + low * high))
                    chosen = jnp.where(match, power, 0.0)
                    for k in range(quarter // 8):
                        loss_sum = loss_sum + terms[k * 8 : (k + 1) * 8]
                    for k in range(PIECE // 8):
                        own_sum = own_sum + chosen[k * 8 : (k + 1) * 8]
        if core and n:
            put_shares(ORDER[n - 1])
    if core:
        put_shares(ORDER[-1])
    loss = loss_sum - LN2 * own_sum
    if core:
        total = jnp.sum(loss + loss_in[...], keepdims=True) * loss_scale
        loss_ref[...] = jnp.broadcast_to(total, loss_ref.shape)
    else:
        loss_ref[...] = loss


def text_shares(coeff_ref, left, image_refs):
    rows = image_refs[0].shape[0]
    part = None
    for r, image_ref in enumerate(image_refs):
        more = lax.dot_general(
            coeff_ref[r * rows : (r + 1) * rows, left : left + rows],
            image_ref[...],
            TN,
            preferred_element_type=jnp.float32,
        )
        part = more if part is None else part + more
    return part


def logit_terms(scalars, images, texts, core=0, loss=None, loss_scale=None):
    rows, depth = images[0].shape
    height, count = len(images) * rows, len(texts) * rows
    coeff, loss_tile = shape_of(height, count, jnp.bfloat16), shape_of(8, PIECE, jnp.float32)
    shares = [shape_of(2 * rows, depth, jnp.bfloat16)] * 2 if core else []
    operands = (*scalars, *images, *texts) + ((loss,) if core else ())
    out_shape = [coeff, *shares, loss_tile]
    outs = pl.pallas_call(
        functools.partial(logit_kernel, core, loss_scale),
        out_shape=out_shape,
        in_specs=[SMEM] + [VMEM] * (len(operands) - 1),
        out_specs=[VMEM] * len(out_shape),
        compiler_params=pltpu.CompilerParams(vmem_limit_bytes=PAIR_VMEM),
        cost_estimate=cost((2 if core else 1) * height * count * depth),
        name="other_logits" if core else "own_logits",
    )(*operands)
    return outs[0], outs[1:-1], outs[-1]


def cost(multiplies):
    return pl.CostEstimate(flops=2 * multiplies, bytes_accessed=8 * 2**20, transcendentals=0)


def text_kernel(first, coeff_ref, came_ref, *refs):
    image_refs, outs = refs[:4], refs[4:]
    rows = outs[0].shape[0]
    for k in (1, 0):
        total = text_shares(coeff_ref, first + k * rows, image_refs) + decode(came_ref[k * rows : (k + 1) * rows, :])
        outs[k][...] = total if outs[k].dtype == jnp.float32 else encode(total)


def text_terms(first, dtype, coeff, came, images):
    rows, depth = images[0].shape
    return pl.pallas_call(
        functools.partial(text_kernel, first),
        out_shape=[shape_of(rows, depth, dtype)] * 2,
        in_specs=[VMEM] * 6,
        out_specs=[VMEM] * 2,
        compiler_params=pltpu.CompilerParams(vmem_limit_bytes=PAIR_VMEM),
        cost_estimate=cost(2 * rows * coeff.shape[0] * depth),
        name="text_terms",
    )(coeff, came, *images)


def image_kernel(first, own_ref, other_ref, *refs):
    text_refs, outs = refs[:8], refs[8:]
    rows = outs[0].shape[0]
    for k, out in enumerate(outs):
        top = first + k * rows
        total = None
        for t, text_ref in enumerate(text_refs):
            coeff_ref, left = (own_ref, other_ref)[t // 4], t % 4 * rows
            more = jnp.dot(
                coeff_ref[top : top + rows, left : left + rows], text_ref[...], preferred_element_type=jnp.float32
            )
            total = more if total is None else total + more
        out[...] = total if out.dtype == jnp.float32 else encode(total)


def image_terms(first, count, dtype, coeffs, texts):
    rows, depth = texts[0].shape
    return pl.pallas_call(
        functools.partial(image_kernel, first),
        out_shape=[shape_of(rows, depth, dtype)] * count,
        in_specs=[VMEM] * 10,
        out_specs=[VMEM] * count,
        compiler_params=pltpu.CompilerParams(vmem_limit_bytes=PAIR_VMEM),
        cost_estimate=cost(2 * count * rows * coeffs[0].shape[1] * depth),
        name="image_terms",
    )(*coeffs, *texts)


def small_call(kernel, name, out_shape, operands):
    return pl.pallas_call(
        kernel,
        out_shape=out_shape,
        in_specs=[VMEM] * len(operands),
        out_specs=[VMEM] * len(out_shape),
        compiler_params=pltpu.CompilerParams(vmem_limit_bytes=SMALL_VMEM),
        name=name,
    )(*operands)


def fold_kernel(own_ref, came_ref, kept, sent):
    sent[...] = encode(own_ref[PIECE:, :] + decode(came_ref[PIECE:, :]))
    kept[...] = own_ref[:PIECE, :] + decode(came_ref[:PIECE, :])


def fold(own, came):
    depth = own.shape[1]
    out_shape = [shape_of(PIECE, depth, jnp.float32), shape_of(PIECE, depth, jnp.bfloat16)]
    return small_call(fold_kernel, "fold", out_shape, (own, came))


def add_kernel(own_ref, came_ref, out_ref):
    out_ref[...] = encode(own_ref[...] + decode(came_ref[...]))


def add_codes(own, came):
    return small_call(add_kernel, "add_codes", [shape_of(*own.shape, jnp.bfloat16)], (own, came))[0]


def finish_kernel(raw_ref, own_ref, ring_ref, far_ref, loss_ref, loss_in, out_ref, loss_out):
    loss_out[0] = jnp.max(loss_ref[...] + loss_in[...])
    grad = own_ref[...] + decode(ring_ref[...]) + decode(far_ref[...])
    wide = raw_ref[...].astype(jnp.float32)
    inverse = lax.rsqrt(jnp.sum(wide * wide, axis=1, keepdims=True) + 1e-06)
    unit = wide * inverse
    out_ref[...] = inverse * (grad - unit * jnp.sum(unit * grad, axis=1, keepdims=True))


def finish(raw, own, ring, far, loss, loss_in):
    return pl.pallas_call(
        finish_kernel,
        out_shape=[shape_of(*raw.shape, jnp.float32), jax.ShapeDtypeStruct((1,), jnp.float32)],
        in_specs=[VMEM] * 6,
        out_specs=[VMEM, SMEM],
        compiler_params=pltpu.CompilerParams(vmem_limit_bytes=SMALL_VMEM),
        name="finish",
    )(raw, own, ring, far, loss, loss_in)


def stack_kernel(first_ref, second_ref, out_ref):
    out_ref[:PIECE, :] = first_ref[...]
    out_ref[PIECE:, :] = second_ref[...]


def stack(first, second):
    return small_call(stack_kernel, "stack", [shape_of(2 * PIECE, *first.shape[1:], first.dtype)], (first, second))[0]


def gather(image, text, scalars):
    groups = ((image, IMAGE_PAIRS), (text, TEXT_PAIRS))
    far = [swap(raw, pairs["x"]) for raw, pairs in groups]
    image, text = unit_rows(image, text)
    *far, scalars = lax.optimization_barrier((*far, scalars))
    far = small_call(far_kernel, "far_units", [shape_of(*part.shape, part.dtype) for part in far], far)
    groups = ((image, IMAGE_PAIRS), (text, TEXT_PAIRS))
    far = [jnp.concatenate([part, swap(part, pairs["z"])], axis=0) for part, (_, pairs) in zip(far, groups)]
    near = [stack(unit, swap(unit, pairs["y"])) for unit, pairs in groups]
    far_late = [swap(part, pairs["y"]) for part, (_, pairs) in zip(far, groups)]
    near_late = [swap(part, pairs["z"]) for part, (_, pairs) in zip(near, groups)]
    images, texts = ([near[k], far[k], near_late[k], far_late[k]] for k in range(2))
    late_core = [after(far[1], *near_late, *far_late), *texts[2:]]
    return images, texts + [swap(part, CORE) for part in (near[1], *late_core)], scalars


def after(value, *others):
    return lax.optimization_barrier((value, *others))[0]


def shards(images, texts, logit_scale, bias):
    place = (lax.axis_index("img") * lax.axis_size("txt") + lax.axis_index("txt")).astype(jnp.int32).reshape(1)
    scalars = (place, jnp.exp(logit_scale).reshape(1, 1), (bias * LOG2E).reshape(1, 1))
    image_all, text_all, scalars = gather(images, texts, scalars)
    count = images.shape[0] * lax.axis_size("img") * lax.axis_size("txt")
    own_coeff, _, loss = logit_terms(scalars, image_all, text_all[:4])
    other_coeff, other, loss = logit_terms(scalars, image_all, text_all[4:], CORE, loss, 1.0 / count)
    coeffs = (own_coeff, other_coeff)

    other_late = swap(other[1], CORE)
    other_early = swap(other[0], CORE)
    loss = loss + swap(loss, CORE)
    near_late, far_late = image_terms(4 * PIECE, 2, jnp.bfloat16, coeffs, text_all)
    image_far = swap(far_late, IMAGE_PAIRS["y"])
    image_near = swap(near_late, IMAGE_PAIRS["z"])
    text_near, text_far = text_terms(
        4 * PIECE, jnp.bfloat16, after(own_coeff, loss, near_late, other_early), other_late, image_all
    )
    text_far = swap(text_far, TEXT_PAIRS["y"])
    text_near = swap(text_near, TEXT_PAIRS["z"])
    loss = after(loss, near_late)
    tiles = swap(jnp.broadcast_to(loss[None], (32, *loss.shape)), IMAGE_PAIRS["x"])
    loss = loss + tiles[0]
    near_early, far_early = image_terms(0, 2, jnp.float32, (after(own_coeff, far_late, loss), other_coeff), text_all)
    tiles = swap(jnp.broadcast_to(loss[None], (32, *loss.shape)), TEXT_PAIRS["x"])
    text_early = text_terms(0, jnp.float32, after(own_coeff, near_early), other_early, image_all)

    image_kept, image_sent = fold(far_early, image_far)
    image_far = swap(image_sent, IMAGE_PAIRS["z"])
    loss = after(loss, text_early[0]) + tiles[0]
    loss = loss + swap(loss, IMAGE_PAIRS["y"])
    text_kept, text_sent = fold(text_early[1], after(text_far, loss))
    text_far = swap(text_sent, TEXT_PAIRS["z"])
    image_own, image_sent = fold(near_early, image_near)
    image_near = swap(image_sent, IMAGE_PAIRS["y"])
    text_own, text_sent = fold(text_early[0], text_near)
    text_near = swap(text_sent, TEXT_PAIRS["y"])

    image_sent = add_codes(image_kept, image_far)
    loss = after(loss, text_kept)
    loss = loss + swap(loss, IMAGE_PAIRS["z"])
    loss = loss + swap(loss, TEXT_PAIRS["y"])
    text_sent = add_codes(text_kept, after(text_far, loss))
    last = swap(loss, TEXT_PAIRS["z"])
    image_grad, _ = finish(images, image_own, image_near, swap(image_sent, IMAGE_PAIRS["x"]), loss, loss)
    text_grad, loss = finish(texts, text_own, text_near, swap(text_sent, TEXT_PAIRS["x"]), loss, last)
    return loss, image_grad, text_grad


def solution(mesh):
    placed = (P(("img", "txt"), None), P(("txt", "img"), None), P(), P())
    return jax.shard_map(
        shards,
        mesh=mesh,
        in_specs=placed,
        out_specs=(P(), P(("img", "txt"), None), P(("txt", "img"), None)),
        check_vma=False,
    )
```

```python
import functools

import jax
import jax.numpy as jnp
from jax import lax
from jax.experimental import pallas as pl
from jax.experimental.pallas import tpu as pltpu
from jax.sharding import PartitionSpec as P

IMAGE_PAIRS = {"x": 2 << 3, "y": 1, "z": 4 << 3}
TEXT_PAIRS = {"x": (2 << 3) + 4, "y": 3, "z": 12 << 3}
CORE = 1 << 3
PIECE = 128
ROWS = ("", "y", "x", "xz", "z", "yz", "xy", "xyz")
PAIR_VMEM = 10 * 2**20
SMALL_VMEM = 8 * 2**20
LOG2E = 1.4426950408889634
LN2 = 0.6931471805599453
NT = (((1,), (1,)), ((), ()))
NN = (((1,), (0,)), ((), ()))
TN = (((0,), (0,)), ((), ()))
HBM = pl.BlockSpec(memory_space=pl.ANY)
SMEM = pl.BlockSpec(memory_space=pltpu.SMEM)
VMEM = pl.BlockSpec(memory_space=pltpu.VMEM)


def shape_of(rows, depth, dtype):
    return jax.ShapeDtypeStruct((rows, depth), dtype)


def swap(value, mask):
    axes = ("img", "txt")
    return lax.ppermute(value, axes, [(k ^ mask, k) for k in range(lax.axis_size(axes))])


def encode(value):
    square = value * value
    return ((square * value) * (square * square)).astype(jnp.bfloat16)


def decode(code):
    wide = code.astype(jnp.float32)
    root = jnp.exp2(jnp.log2(jnp.abs(wide)) * (1.0 / 7.0))
    return jnp.where(wide < 0.0, -root, root)


def unit_kernel(images_ref, texts_ref, image_out, text_out, raw, sems):
    loads = [pltpu.make_async_copy(ref, raw.at[k], sems.at[k]) for k, ref in enumerate((images_ref, texts_ref))]
    for load in loads:
        load.start()
    for k, out in enumerate((image_out, text_out)):
        loads[k].wait()
        wide = raw[k].astype(jnp.float32)
        inverse = lax.rsqrt(jnp.sum(wide * wide, axis=1, keepdims=True) + 1e-06)
        out[...] = (wide * inverse).astype(jnp.bfloat16)


def unit_rows(images, texts):
    out = shape_of(*images.shape, jnp.bfloat16)
    return pl.pallas_call(
        unit_kernel,
        out_shape=[out, out],
        in_specs=[HBM, HBM],
        out_specs=[VMEM, VMEM],
        scratch_shapes=[pltpu.VMEM((2, *images.shape), jnp.bfloat16), pltpu.SemaphoreType.DMA((2,))],
        compiler_params=pltpu.CompilerParams(vmem_limit_bytes=60 * 2**20),
        name="unit_rows",
    )(images, texts)


def far_kernel(images_ref, texts_ref, *out_refs):
    for raw_ref, out_ref in zip((images_ref, texts_ref), out_refs):
        wide = raw_ref[...].astype(jnp.float32)
        inverse = lax.rsqrt(jnp.sum(wide * wide, axis=1, keepdims=True) + 1e-06)
        out_ref[...] = (wide * inverse).astype(jnp.bfloat16)


def row_masks(pairs):
    return [sum(pairs[axis] for axis in axes) for axes in ROWS]


ORDER = (2, 3, 0, 1)


def logit_kernel(core, loss_scale, place_ref, temper_ref, shift_ref, *refs):
    image_refs, text_refs = refs[:4], refs[4:8]
    if core:
        loss_in, coeff_ref, other_refs, loss_ref = refs[8], refs[9], refs[10:12], refs[12]
    else:
        coeff_ref, loss_ref = refs[8:]
    rows = image_refs[0].shape[0]
    pieces = rows // PIECE

    place = place_ref[0]
    image_base = [lax.bitwise_xor(place, mask) * PIECE for mask in row_masks(IMAGE_PAIRS)]
    text_base = []
    for mask in row_masks(TEXT_PAIRS):
        flat = lax.bitwise_xor(place, mask ^ core)
        text_base.append((lax.rem(flat, 8) * 16 + lax.div(flat, 8)) * PIECE)

    temper = jnp.broadcast_to(temper_ref[...], (1, PIECE))
    slope = temper * LOG2E
    shift = jnp.broadcast_to(shift_ref[...], (1, PIECE))
    apart = lax.broadcasted_iota(jnp.int32, (PIECE, PIECE), 0) - lax.broadcasted_iota(
        jnp.int32, (PIECE, PIECE), 1
    )
    quarter = PIECE // 4
    loss_sum = jnp.zeros((8, PIECE), jnp.float32)
    own_sum = jnp.zeros((8, PIECE), jnp.float32)
    def put_shares(t):
        other_refs[t // 2][t % 2 * rows : (t % 2 + 1) * rows, :] = encode(
            text_shares(coeff_ref, t * rows, image_refs)
        )

    for n, t in enumerate(ORDER):
        left = t * rows
        for r, image_ref in enumerate(image_refs):
            dots = lax.dot_general(image_ref[...], text_refs[t][...], NT, preferred_element_type=jnp.float32)
            for a in range(pieces):
                top = r * rows + a * PIECE
                for b in range(pieces):
                    power = dots[a * PIECE : (a + 1) * PIECE, b * PIECE : (b + 1) * PIECE] * slope + shift
                    grown = jnp.exp2(power)
                    match = apart == text_base[t * pieces + b] - image_base[r * pieces + a]
                    weight = jnp.where(match, -1.0, grown) * pl.reciprocal(1.0 + grown) * temper
                    column = left + b * PIECE
                    coeff_ref[top : top + PIECE, column : column + PIECE] = weight.astype(jnp.bfloat16)
                    g = [grown[k * quarter : (k + 1) * quarter] for k in range(4)]
                    low = g[0] + g[1] + g[0] * g[1]
                    high = g[2] + g[3] + g[2] * g[3]
                    terms = jnp.log(1.0 + (low + high + low * high))
                    chosen = jnp.where(match, power, 0.0)
                    for k in range(quarter // 8):
                        loss_sum = loss_sum + terms[k * 8 : (k + 1) * 8]
                    for k in range(PIECE // 8):
                        own_sum = own_sum + chosen[k * 8 : (k + 1) * 8]
        if core and n:
            put_shares(ORDER[n - 1])
    if core:
        put_shares(ORDER[-1])
    loss = loss_sum - LN2 * own_sum
    if core:
        total = jnp.sum(loss + loss_in[...], keepdims=True) * loss_scale
        loss_ref[...] = jnp.broadcast_to(total, loss_ref.shape)
    else:
        loss_ref[...] = loss


def text_shares(coeff_ref, left, image_refs):
    rows = image_refs[0].shape[0]
    part = None
    for r, image_ref in enumerate(image_refs):
        more = lax.dot_general(
            coeff_ref[r * rows : (r + 1) * rows, left : left + rows],
            image_ref[...],
            TN,
            preferred_element_type=jnp.float32,
        )
        part = more if part is None else part + more
    return part


def logit_terms(scalars, images, texts, core=0, loss=None, loss_scale=None):
    rows, depth = images[0].shape
    height, count = len(images) * rows, len(texts) * rows
    coeff, loss_tile = shape_of(height, count, jnp.bfloat16), shape_of(8, PIECE, jnp.float32)
    shares = [shape_of(2 * rows, depth, jnp.bfloat16)] * 2 if core else []
    operands = (*scalars, *images, *texts) + ((loss,) if core else ())
    out_shape = [coeff, *shares, loss_tile]
    outs = pl.pallas_call(
        functools.partial(logit_kernel, core, loss_scale),
        out_shape=out_shape,
        in_specs=[SMEM] + [VMEM] * (len(operands) - 1),
        out_specs=[VMEM] * len(out_shape),
        compiler_params=pltpu.CompilerParams(vmem_limit_bytes=PAIR_VMEM),
        cost_estimate=cost((2 if core else 1) * height * count * depth),
        name="other_logits" if core else "own_logits",
    )(*operands)
    return outs[0], outs[1:-1], outs[-1]


def cost(multiplies):
    return pl.CostEstimate(flops=2 * multiplies, bytes_accessed=8 * 2**20, transcendentals=0)


def text_kernel(first, coeff_ref, came_ref, *refs):
    image_refs, outs = refs[:4], refs[4:]
    rows = outs[0].shape[0]
    for k in (1, 0):
        total = text_shares(coeff_ref, first + k * rows, image_refs) + decode(came_ref[k * rows : (k + 1) * rows, :])
        outs[k][...] = total if outs[k].dtype == jnp.float32 else encode(total)


def text_terms(first, dtype, coeff, came, images):
    rows, depth = images[0].shape
    return pl.pallas_call(
        functools.partial(text_kernel, first),
        out_shape=[shape_of(rows, depth, dtype)] * 2,
        in_specs=[VMEM] * 6,
        out_specs=[VMEM] * 2,
        compiler_params=pltpu.CompilerParams(vmem_limit_bytes=PAIR_VMEM),
        cost_estimate=cost(2 * rows * coeff.shape[0] * depth),
        name="text_terms",
    )(coeff, came, *images)


def image_kernel(first, own_ref, other_ref, *refs):
    text_refs, outs = refs[:8], refs[8:]
    rows = outs[0].shape[0]
    for k, out in enumerate(outs):
        top = first + k * rows
        total = None
        for t, text_ref in enumerate(text_refs):
            coeff_ref, left = (own_ref, other_ref)[t // 4], t % 4 * rows
            more = jnp.dot(
                coeff_ref[top : top + rows, left : left + rows], text_ref[...], preferred_element_type=jnp.float32
            )
            total = more if total is None else total + more
        out[...] = total if out.dtype == jnp.float32 else encode(total)


def image_terms(first, count, dtype, coeffs, texts):
    rows, depth = texts[0].shape
    return pl.pallas_call(
        functools.partial(image_kernel, first),
        out_shape=[shape_of(rows, depth, dtype)] * count,
        in_specs=[VMEM] * 10,
        out_specs=[VMEM] * count,
        compiler_params=pltpu.CompilerParams(vmem_limit_bytes=PAIR_VMEM),
        cost_estimate=cost(2 * count * rows * coeffs[0].shape[1] * depth),
        name="image_terms",
    )(*coeffs, *texts)


def small_call(kernel, name, out_shape, operands):
    return pl.pallas_call(
        kernel,
        out_shape=out_shape,
        in_specs=[VMEM] * len(operands),
        out_specs=[VMEM] * len(out_shape),
        compiler_params=pltpu.CompilerParams(vmem_limit_bytes=SMALL_VMEM),
        name=name,
    )(*operands)


def fold_kernel(own_ref, came_ref, kept, sent):
    sent[...] = encode(own_ref[PIECE:, :] + decode(came_ref[PIECE:, :]))
    kept[...] = own_ref[:PIECE, :] + decode(came_ref[:PIECE, :])


def fold(own, came):
    depth = own.shape[1]
    out_shape = [shape_of(PIECE, depth, jnp.float32), shape_of(PIECE, depth, jnp.bfloat16)]
    return small_call(fold_kernel, "fold", out_shape, (own, came))


def add_kernel(own_ref, came_ref, out_ref):
    out_ref[...] = encode(own_ref[...] + decode(came_ref[...]))


def add_codes(own, came):
    return small_call(add_kernel, "add_codes", [shape_of(*own.shape, jnp.bfloat16)], (own, came))[0]


def finish_kernel(raw_ref, own_ref, ring_ref, far_ref, loss_ref, loss_in, out_ref, loss_out):
    loss_out[0] = jnp.max(loss_ref[...] + loss_in[...])
    grad = own_ref[...] + decode(ring_ref[...]) + decode(far_ref[...])
    wide = raw_ref[...].astype(jnp.float32)
    inverse = lax.rsqrt(jnp.sum(wide * wide, axis=1, keepdims=True) + 1e-06)
    unit = wide * inverse
    out_ref[...] = inverse * (grad - unit * jnp.sum(unit * grad, axis=1, keepdims=True))


def finish(raw, own, ring, far, loss, loss_in):
    return pl.pallas_call(
        finish_kernel,
        out_shape=[shape_of(*raw.shape, jnp.float32), jax.ShapeDtypeStruct((1,), jnp.float32)],
        in_specs=[VMEM] * 6,
        out_specs=[VMEM, SMEM],
        compiler_params=pltpu.CompilerParams(vmem_limit_bytes=SMALL_VMEM),
        name="finish",
    )(raw, own, ring, far, loss, loss_in)


def stack_kernel(first_ref, second_ref, out_ref):
    out_ref[:PIECE, :] = first_ref[...]
    out_ref[PIECE:, :] = second_ref[...]


def stack(first, second):
    return small_call(stack_kernel, "stack", [shape_of(2 * PIECE, *first.shape[1:], first.dtype)], (first, second))[0]


def gather(image, text, scalars):
    groups = ((image, IMAGE_PAIRS), (text, TEXT_PAIRS))
    far = [swap(raw, pairs["x"]) for raw, pairs in groups]
    image, text = unit_rows(image, text)
    *far, scalars = lax.optimization_barrier((*far, scalars))
    far = small_call(far_kernel, "far_units", [shape_of(*part.shape, part.dtype) for part in far], far)
    groups = ((image, IMAGE_PAIRS), (text, TEXT_PAIRS))
    far = [jnp.concatenate([part, swap(part, pairs["z"])], axis=0) for part, (_, pairs) in zip(far, groups)]
    near = [stack(unit, swap(unit, pairs["y"])) for unit, pairs in groups]
    far_late = [swap(part, pairs["y"]) for part, (_, pairs) in zip(far, groups)]
    near_late = [swap(part, pairs["z"]) for part, (_, pairs) in zip(near, groups)]
    images, texts = ([near[k], far[k], near_late[k], far_late[k]] for k in range(2))
    late_core = [after(far[1], *near_late, *far_late), *texts[2:]]
    return images, texts + [swap(part, CORE) for part in (near[1], *late_core)], scalars


def after(value, *others):
    return lax.optimization_barrier((value, *others))[0]


def shards(images, texts, logit_scale, bias):
    place = (lax.axis_index("img") * lax.axis_size("txt") + lax.axis_index("txt")).astype(jnp.int32).reshape(1)
    scalars = (place, jnp.exp(logit_scale).reshape(1, 1), (bias * LOG2E).reshape(1, 1))
    image_all, text_all, scalars = gather(images, texts, scalars)
    count = images.shape[0] * lax.axis_size("img") * lax.axis_size("txt")
    own_coeff, _, loss = logit_terms(scalars, image_all, text_all[:4])
    other_coeff, other, loss = logit_terms(scalars, image_all, text_all[4:], CORE, loss, 1.0 / count)
    coeffs = (own_coeff, other_coeff)

    other_late = swap(other[1], CORE)
    other_early = swap(other[0], CORE)
    loss = loss + swap(loss, CORE)
    near_late, far_late = image_terms(4 * PIECE, 2, jnp.bfloat16, coeffs, text_all)
    image_far = swap(far_late, IMAGE_PAIRS["y"])
    image_near = swap(near_late, IMAGE_PAIRS["z"])
    text_near, text_far = text_terms(
        4 * PIECE, jnp.bfloat16, after(own_coeff, loss, near_late, other_early), other_late, image_all
    )
    text_far = swap(text_far, TEXT_PAIRS["y"])
    text_near = swap(text_near, TEXT_PAIRS["z"])
    loss = after(loss, near_late)
    tiles = swap(jnp.broadcast_to(loss[None], (24, *loss.shape)), IMAGE_PAIRS["x"])
    loss = loss + tiles[0]
    near_early, far_early = image_terms(0, 2, jnp.float32, (after(own_coeff, far_late, loss), other_coeff), text_all)
    tiles = swap(jnp.broadcast_to(loss[None], (24, *loss.shape)), TEXT_PAIRS["x"])
    text_early = text_terms(0, jnp.float32, after(own_coeff, near_early), other_early, image_all)

    image_kept, image_sent = fold(far_early, image_far)
    image_far = swap(image_sent, IMAGE_PAIRS["z"])
    loss = after(loss, text_early[0]) + tiles[0]
    loss = loss + swap(loss, IMAGE_PAIRS["y"])
    text_kept, text_sent = fold(text_early[1], after(text_far, loss))
    text_far = swap(text_sent, TEXT_PAIRS["z"])
    image_own, image_sent = fold(near_early, image_near)
    image_near = swap(image_sent, IMAGE_PAIRS["y"])
    text_own, text_sent = fold(text_early[0], text_near)
    text_near = swap(text_sent, TEXT_PAIRS["y"])

    image_sent = add_codes(image_kept, image_far)
    loss = after(loss, text_kept)
    loss = loss + swap(loss, IMAGE_PAIRS["z"])
    loss = loss + swap(loss, TEXT_PAIRS["y"])
    text_sent = add_codes(text_kept, after(text_far, loss))
    last = swap(loss, TEXT_PAIRS["z"])
    image_grad, _ = finish(images, image_own, image_near, swap(image_sent, IMAGE_PAIRS["x"]), loss, loss)
    text_grad, loss = finish(texts, text_own, text_near, swap(text_sent, TEXT_PAIRS["x"]), loss, last)
    return loss, image_grad, text_grad


def solution(mesh):
    placed = (P(("img", "txt"), None), P(("txt", "img"), None), P(), P())
    return jax.shard_map(
        shards,
        mesh=mesh,
        in_specs=placed,
        out_specs=(P(), P(("img", "txt"), None), P(("txt", "img"), None)),
        check_vma=False,
    )
```

```python
import functools

import jax
import jax.numpy as jnp
from jax import lax
from jax.experimental import pallas as pl
from jax.experimental.pallas import tpu as pltpu
from jax.sharding import PartitionSpec as P

IMAGE_PAIRS = {"x": 2 << 3, "y": 1, "z": 4 << 3}
TEXT_PAIRS = {"x": (2 << 3) + 4, "y": 3, "z": 12 << 3}
CORE = 1 << 3
PIECE = 128
ROWS = ("", "y", "x", "xz", "z", "yz", "xy", "xyz")
PAIR_VMEM = 10 * 2**20
SMALL_VMEM = 8 * 2**20
LOG2E = 1.4426950408889634
LN2 = 0.6931471805599453
NT = (((1,), (1,)), ((), ()))
NN = (((1,), (0,)), ((), ()))
TN = (((0,), (0,)), ((), ()))
HBM = pl.BlockSpec(memory_space=pl.ANY)
SMEM = pl.BlockSpec(memory_space=pltpu.SMEM)
VMEM = pl.BlockSpec(memory_space=pltpu.VMEM)


def shape_of(rows, depth, dtype):
    return jax.ShapeDtypeStruct((rows, depth), dtype)


def swap(value, mask):
    axes = ("img", "txt")
    return lax.ppermute(value, axes, [(k ^ mask, k) for k in range(lax.axis_size(axes))])


def encode(value):
    square = value * value
    return ((square * value) * (square * square)).astype(jnp.bfloat16)


def decode(code):
    wide = code.astype(jnp.float32)
    root = jnp.exp2(jnp.log2(jnp.abs(wide)) * (1.0 / 7.0))
    return jnp.where(wide < 0.0, -root, root)


def unit_kernel(images_ref, texts_ref, image_out, text_out, raw, sems):
    loads = [pltpu.make_async_copy(ref, raw.at[k], sems.at[k]) for k, ref in enumerate((images_ref, texts_ref))]
    for load in loads:
        load.start()
    for k, out in enumerate((image_out, text_out)):
        loads[k].wait()
        wide = raw[k].astype(jnp.float32)
        inverse = lax.rsqrt(jnp.sum(wide * wide, axis=1, keepdims=True) + 1e-06)
        out[...] = (wide * inverse).astype(jnp.bfloat16)


def unit_rows(images, texts):
    out = shape_of(*images.shape, jnp.bfloat16)
    return pl.pallas_call(
        unit_kernel,
        out_shape=[out, out],
        in_specs=[HBM, HBM],
        out_specs=[VMEM, VMEM],
        scratch_shapes=[pltpu.VMEM((2, *images.shape), jnp.bfloat16), pltpu.SemaphoreType.DMA((2,))],
        compiler_params=pltpu.CompilerParams(vmem_limit_bytes=60 * 2**20),
        name="unit_rows",
    )(images, texts)


def far_kernel(images_ref, texts_ref, *out_refs):
    for raw_ref, out_ref in zip((images_ref, texts_ref), out_refs):
        wide = raw_ref[...].astype(jnp.float32)
        inverse = lax.rsqrt(jnp.sum(wide * wide, axis=1, keepdims=True) + 1e-06)
        out_ref[...] = (wide * inverse).astype(jnp.bfloat16)


def row_masks(pairs):
    return [sum(pairs[axis] for axis in axes) for axes in ROWS]


ORDER = (2, 3, 0, 1)


def logit_kernel(core, loss_scale, place_ref, temper_ref, shift_ref, *refs):
    image_refs, text_refs = refs[:4], refs[4:8]
    if core:
        loss_in, coeff_ref, other_refs, loss_ref = refs[8], refs[9], refs[10:12], refs[12]
    else:
        coeff_ref, loss_ref = refs[8:]
    rows = image_refs[0].shape[0]
    pieces = rows // PIECE

    place = place_ref[0]
    image_base = [lax.bitwise_xor(place, mask) * PIECE for mask in row_masks(IMAGE_PAIRS)]
    text_base = []
    for mask in row_masks(TEXT_PAIRS):
        flat = lax.bitwise_xor(place, mask ^ core)
        text_base.append((lax.rem(flat, 8) * 16 + lax.div(flat, 8)) * PIECE)

    temper = jnp.broadcast_to(temper_ref[...], (1, PIECE))
    slope = temper * LOG2E
    shift = jnp.broadcast_to(shift_ref[...], (1, PIECE))
    apart = lax.broadcasted_iota(jnp.int32, (PIECE, PIECE), 0) - lax.broadcasted_iota(
        jnp.int32, (PIECE, PIECE), 1
    )
    quarter = PIECE // 4
    loss_sum = jnp.zeros((8, PIECE), jnp.float32)
    own_sum = jnp.zeros((8, PIECE), jnp.float32)
    def put_shares(t):
        other_refs[t // 2][t % 2 * rows : (t % 2 + 1) * rows, :] = encode(
            text_shares(coeff_ref, t * rows, image_refs)
        )

    for n, t in enumerate(ORDER):
        left = t * rows
        for r, image_ref in enumerate(image_refs):
            dots = lax.dot_general(image_ref[...], text_refs[t][...], NT, preferred_element_type=jnp.float32)
            for a in range(pieces):
                top = r * rows + a * PIECE
                for b in range(pieces):
                    power = dots[a * PIECE : (a + 1) * PIECE, b * PIECE : (b + 1) * PIECE] * slope + shift
                    grown = jnp.exp2(power)
                    match = apart == text_base[t * pieces + b] - image_base[r * pieces + a]
                    weight = jnp.where(match, -1.0, grown) * pl.reciprocal(1.0 + grown) * temper
                    column = left + b * PIECE
                    coeff_ref[top : top + PIECE, column : column + PIECE] = weight.astype(jnp.bfloat16)
                    g = [grown[k * quarter : (k + 1) * quarter] for k in range(4)]
                    low = g[0] + g[1] + g[0] * g[1]
                    high = g[2] + g[3] + g[2] * g[3]
                    terms = jnp.log(1.0 + (low + high + low * high))
                    chosen = jnp.where(match, power, 0.0)
                    for k in range(quarter // 8):
                        loss_sum = loss_sum + terms[k * 8 : (k + 1) * 8]
                    for k in range(PIECE // 8):
                        own_sum = own_sum + chosen[k * 8 : (k + 1) * 8]
        if core and n:
            put_shares(ORDER[n - 1])
    if core:
        put_shares(ORDER[-1])
    loss = loss_sum - LN2 * own_sum
    if core:
        total = jnp.sum(loss + loss_in[...], keepdims=True) * loss_scale
        loss_ref[...] = jnp.broadcast_to(total, loss_ref.shape)
    else:
        loss_ref[...] = loss


def text_shares(coeff_ref, left, image_refs):
    rows = image_refs[0].shape[0]
    part = None
    for r, image_ref in enumerate(image_refs):
        more = lax.dot_general(
            coeff_ref[r * rows : (r + 1) * rows, left : left + rows],
            image_ref[...],
            TN,
            preferred_element_type=jnp.float32,
        )
        part = more if part is None else part + more
    return part


def logit_terms(scalars, images, texts, core=0, loss=None, loss_scale=None):
    rows, depth = images[0].shape
    height, count = len(images) * rows, len(texts) * rows
    coeff, loss_tile = shape_of(height, count, jnp.bfloat16), shape_of(8, PIECE, jnp.float32)
    shares = [shape_of(2 * rows, depth, jnp.bfloat16)] * 2 if core else []
    operands = (*scalars, *images, *texts) + ((loss,) if core else ())
    out_shape = [coeff, *shares, loss_tile]
    outs = pl.pallas_call(
        functools.partial(logit_kernel, core, loss_scale),
        out_shape=out_shape,
        in_specs=[SMEM] + [VMEM] * (len(operands) - 1),
        out_specs=[VMEM] * len(out_shape),
        compiler_params=pltpu.CompilerParams(vmem_limit_bytes=PAIR_VMEM),
        cost_estimate=cost((2 if core else 1) * height * count * depth),
        name="other_logits" if core else "own_logits",
    )(*operands)
    return outs[0], outs[1:-1], outs[-1]


def cost(multiplies):
    return pl.CostEstimate(flops=2 * multiplies, bytes_accessed=8 * 2**20, transcendentals=0)


def text_kernel(first, coeff_ref, came_ref, *refs):
    image_refs, outs = refs[:4], refs[4:]
    rows = outs[0].shape[0]
    for k in (1, 0):
        total = text_shares(coeff_ref, first + k * rows, image_refs) + decode(came_ref[k * rows : (k + 1) * rows, :])
        outs[k][...] = total if outs[k].dtype == jnp.float32 else encode(total)


def text_terms(first, dtype, coeff, came, images):
    rows, depth = images[0].shape
    return pl.pallas_call(
        functools.partial(text_kernel, first),
        out_shape=[shape_of(rows, depth, dtype)] * 2,
        in_specs=[VMEM] * 6,
        out_specs=[VMEM] * 2,
        compiler_params=pltpu.CompilerParams(vmem_limit_bytes=PAIR_VMEM),
        cost_estimate=cost(2 * rows * coeff.shape[0] * depth),
        name="text_terms",
    )(coeff, came, *images)


def image_kernel(first, own_ref, other_ref, *refs):
    text_refs, outs = refs[:8], refs[8:]
    rows = outs[0].shape[0]
    for k, out in enumerate(outs):
        top = first + k * rows
        total = None
        for t, text_ref in enumerate(text_refs):
            coeff_ref, left = (own_ref, other_ref)[t // 4], t % 4 * rows
            more = jnp.dot(
                coeff_ref[top : top + rows, left : left + rows], text_ref[...], preferred_element_type=jnp.float32
            )
            total = more if total is None else total + more
        out[...] = total if out.dtype == jnp.float32 else encode(total)


def image_terms(first, count, dtype, coeffs, texts):
    rows, depth = texts[0].shape
    return pl.pallas_call(
        functools.partial(image_kernel, first),
        out_shape=[shape_of(rows, depth, dtype)] * count,
        in_specs=[VMEM] * 10,
        out_specs=[VMEM] * count,
        compiler_params=pltpu.CompilerParams(vmem_limit_bytes=PAIR_VMEM),
        cost_estimate=cost(2 * count * rows * coeffs[0].shape[1] * depth),
        name="image_terms",
    )(*coeffs, *texts)


def small_call(kernel, name, out_shape, operands):
    return pl.pallas_call(
        kernel,
        out_shape=out_shape,
        in_specs=[VMEM] * len(operands),
        out_specs=[VMEM] * len(out_shape),
        compiler_params=pltpu.CompilerParams(vmem_limit_bytes=SMALL_VMEM),
        name=name,
    )(*operands)


def fold_kernel(own_ref, came_ref, kept, sent):
    sent[...] = encode(own_ref[PIECE:, :] + decode(came_ref[PIECE:, :]))
    kept[...] = own_ref[:PIECE, :] + decode(came_ref[:PIECE, :])


def fold(own, came):
    depth = own.shape[1]
    out_shape = [shape_of(PIECE, depth, jnp.float32), shape_of(PIECE, depth, jnp.bfloat16)]
    return small_call(fold_kernel, "fold", out_shape, (own, came))


def add_kernel(own_ref, came_ref, out_ref):
    out_ref[...] = encode(own_ref[...] + decode(came_ref[...]))


def add_codes(own, came):
    return small_call(add_kernel, "add_codes", [shape_of(*own.shape, jnp.bfloat16)], (own, came))[0]


def finish_kernel(raw_ref, own_ref, ring_ref, far_ref, loss_ref, loss_in, out_ref, loss_out):
    loss_out[0] = jnp.max(loss_ref[...] + loss_in[...])
    grad = own_ref[...] + decode(ring_ref[...]) + decode(far_ref[...])
    wide = raw_ref[...].astype(jnp.float32)
    inverse = lax.rsqrt(jnp.sum(wide * wide, axis=1, keepdims=True) + 1e-06)
    unit = wide * inverse
    out_ref[...] = inverse * (grad - unit * jnp.sum(unit * grad, axis=1, keepdims=True))


def finish(raw, own, ring, far, loss, loss_in):
    return pl.pallas_call(
        finish_kernel,
        out_shape=[shape_of(*raw.shape, jnp.float32), jax.ShapeDtypeStruct((1,), jnp.float32)],
        in_specs=[VMEM] * 6,
        out_specs=[VMEM, SMEM],
        compiler_params=pltpu.CompilerParams(vmem_limit_bytes=SMALL_VMEM),
        name="finish",
    )(raw, own, ring, far, loss, loss_in)


def stack_kernel(first_ref, second_ref, out_ref):
    out_ref[:PIECE, :] = first_ref[...]
    out_ref[PIECE:, :] = second_ref[...]


def stack(first, second):
    return small_call(stack_kernel, "stack", [shape_of(2 * PIECE, *first.shape[1:], first.dtype)], (first, second))[0]


def gather(image, text, scalars):
    groups = ((image, IMAGE_PAIRS), (text, TEXT_PAIRS))
    far = [swap(raw, pairs["x"]) for raw, pairs in groups]
    image, text = unit_rows(image, text)
    *far, scalars = lax.optimization_barrier((*far, scalars))
    far = small_call(far_kernel, "far_units", [shape_of(*part.shape, part.dtype) for part in far], far)
    groups = ((image, IMAGE_PAIRS), (text, TEXT_PAIRS))
    far = [jnp.concatenate([part, swap(part, pairs["z"])], axis=0) for part, (_, pairs) in zip(far, groups)]
    near = [stack(unit, swap(unit, pairs["y"])) for unit, pairs in groups]
    far_late = [swap(part, pairs["y"]) for part, (_, pairs) in zip(far, groups)]
    near_late = [swap(part, pairs["z"]) for part, (_, pairs) in zip(near, groups)]
    images, texts = ([near[k], far[k], near_late[k], far_late[k]] for k in range(2))
    late_core = [after(far[1], *near_late, *far_late), *texts[2:]]
    return images, texts + [swap(part, CORE) for part in (near[1], *late_core)], scalars


def after(value, *others):
    return lax.optimization_barrier((value, *others))[0]


def shards(images, texts, logit_scale, bias):
    place = (lax.axis_index("img") * lax.axis_size("txt") + lax.axis_index("txt")).astype(jnp.int32).reshape(1)
    scalars = (place, jnp.exp(logit_scale).reshape(1, 1), (bias * LOG2E).reshape(1, 1))
    image_all, text_all, scalars = gather(images, texts, scalars)
    count = images.shape[0] * lax.axis_size("img") * lax.axis_size("txt")
    own_coeff, _, loss = logit_terms(scalars, image_all, text_all[:4])
    other_coeff, other, loss = logit_terms(scalars, image_all, text_all[4:], CORE, loss, 1.0 / count)
    coeffs = (own_coeff, other_coeff)

    other_late = swap(other[1], CORE)
    other_early = swap(other[0], CORE)
    loss = loss + swap(loss, CORE)
    near_late, far_late = image_terms(4 * PIECE, 2, jnp.bfloat16, coeffs, text_all)
    image_far = swap(far_late, IMAGE_PAIRS["y"])
    image_near = swap(near_late, IMAGE_PAIRS["z"])
    text_near, text_far = text_terms(
        4 * PIECE, jnp.bfloat16, after(own_coeff, loss, near_late, other_early), other_late, image_all
    )
    text_far = swap(text_far, TEXT_PAIRS["y"])
    text_near = swap(text_near, TEXT_PAIRS["z"])
    loss = after(loss, near_late)
    tiles = swap(jnp.broadcast_to(loss[None], (16, *loss.shape)), IMAGE_PAIRS["x"])
    loss = loss + tiles[0]
    near_early, far_early = image_terms(0, 2, jnp.float32, (after(own_coeff, far_late, loss), other_coeff), text_all)
    tiles = swap(jnp.broadcast_to(loss[None], (16, *loss.shape)), TEXT_PAIRS["x"])
    text_early = text_terms(0, jnp.float32, after(own_coeff, near_early), other_early, image_all)

    image_kept, image_sent = fold(far_early, image_far)
    image_far = swap(image_sent, IMAGE_PAIRS["z"])
    loss = after(loss, text_early[0]) + tiles[0]
    loss = loss + swap(loss, IMAGE_PAIRS["y"])
    text_kept, text_sent = fold(text_early[1], after(text_far, loss))
    text_far = swap(text_sent, TEXT_PAIRS["z"])
    image_own, image_sent = fold(near_early, image_near)
    image_near = swap(image_sent, IMAGE_PAIRS["y"])
    text_own, text_sent = fold(text_early[0], text_near)
    text_near = swap(text_sent, TEXT_PAIRS["y"])

    image_sent = add_codes(image_kept, image_far)
    loss = after(loss, text_kept)
    loss = loss + swap(loss, IMAGE_PAIRS["z"])
    loss = loss + swap(loss, TEXT_PAIRS["y"])
    text_sent = add_codes(text_kept, after(text_far, loss))
    last = swap(loss, TEXT_PAIRS["z"])
    image_grad, _ = finish(images, image_own, image_near, swap(image_sent, IMAGE_PAIRS["x"]), loss, loss)
    text_grad, loss = finish(texts, text_own, text_near, swap(text_sent, TEXT_PAIRS["x"]), loss, last)
    return loss, image_grad, text_grad


def solution(mesh):
    placed = (P(("img", "txt"), None), P(("txt", "img"), None), P(), P())
    return jax.shard_map(
        shards,
        mesh=mesh,
        in_specs=placed,
        out_specs=(P(), P(("img", "txt"), None), P(("txt", "img"), None)),
        check_vma=False,
    )
```
